256 devices in a mesh: order: 8 (over z_lo, core), lat: 32 (over y, x, z_hi).
Axes of the slice: x: 4, y: 4, z: 8 (z_hi: 2, z_lo: 4; z = z_hi * 4 + z_lo), core: 2. Of those that a mesh axis runs over, the one named last changes fastest.
Arguments:
- control: float32 [2, 3, 2, 1280, 1280], P(None, None, None, ('order', 'lat')), may hold values from -6 to 6
- vertical: float32 [3, 2, 2, 1280], replicated, may hold values from -4 to 4
- legendre: bfloat16 [1280, 1280, 640], P(('order', 'lat')), may hold values from -0.0034179688 to 0.0034179688
- order_assign: int32 [1280], replicated, may hold values from 0 to 1279, each once
- send_list: int32 [8, 32, 256], P('order', 'lat'), may hold values from 0 to 199
- used_slot_counts: int32 [8, 32, 32], P('order', 'lat'), may hold values from 1 to 8, as said below
- obs_count: int32 [8, 32, 256], P('order', 'lat'), may hold values from 1 to 16
- obs_var: int32 [8, 32, 4096], P('order', 'lat'), may hold values from 0 to 5
- obs_col: int32 [8, 32, 4096], P('order', 'lat'), may hold values from 0 to 60
- obs_weight: float32 [4, 8, 32, 4096], P(None, 'order', 'lat'), may hold values from 0.1 to 0.9
- obs_value: float32 [8, 32, 4096], P('order', 'lat'), may hold values from -6 to 6
- obs_error: float32 [8, 32, 4096], P('order', 'lat'), may hold values from 0.1 to 1
Outputs:
- increment: bfloat16 [1280, 6, 2560], P(('order', 'lat'))
- weighted: float32 [8, 32, 4096], P('order', 'lat')
- gradient: float32 [2, 3, 2, 1280, 1280], P(None, None, None, ('order', 'lat'))
The draws below stay inside these ranges and needn't reach their ends.
Inputs may be any that keep to these rules, and one draw needn't show every extreme that they name: `send_list`: entries for slots t >= used_slot_counts[o, d, s] are not read. `used_slot_counts`: in every order group one owner receives 8 blocks from every source device. `order_assign`: each order once.
All inputs are finite; a program needn't handle non-finite values.
Results may differ from the reference program's by a relative error of at most 0.0062.
Values may be sent and summed in bfloat16 or wider, within the bound.
No kernel may reach another device: no remote copies, remote signals or barrier semaphores. Data moves between devices by JAX's collectives and lax.ppermute only.
A program may use at most 128 MiB of HBM per device.

```python
import math
import jax
import jax.numpy as jnp
from jax import lax

MM = 1280
NLON = 2560
FIELDS = 3
LEV = 2
BLKW = 64
CAP = 8
KOBS = 16
NHALF = 640
VARS = 6
BLOCKS_DEV = 200
OBSERVATION_SLOTS = 4096
N_ORDER = 8
N_LAT = 32


def draw_used_slot_counts(key, part):
    keys = jax.random.split(key, 3)
    busiest = jax.random.randint(keys[0], (N_ORDER, 1, 1), 0, N_LAT)
    reach = jax.random.randint(keys[1], (N_ORDER, N_LAT, 1), 1, CAP + 1)
    counts = jax.random.randint(keys[2], (N_ORDER, N_LAT, N_LAT), 1, reach + 1)
    owners = lax.broadcasted_iota(jnp.int32, (N_ORDER, N_LAT, N_LAT), 1)
    return jnp.where(owners == busiest, CAP, counts).astype(jnp.int32)


def set_ends(entries, stream_key, low, top_value):
    longest = entries.shape.index(max(entries.shape))
    spots = []
    for shift in (0, 1):
        where = [jax.random.randint(jax.random.fold_in(stream_key, axis), (), 0, length) for axis, length in enumerate(entries.shape)]
        where[longest] = (where[longest] + shift) % entries.shape[longest]
        spots.append(tuple(where))
    return entries.at[spots[0]].set(low).at[spots[1]].set(top_value)


def block_scale(own_key, dims, shards, smallest, top_value):
    loudness, own = 1.0, jax.random.fold_in(own_key, 6)
    for axis_at, parts in shards:
        draws = jnp.exp(jax.random.uniform(jax.random.fold_in(own, axis_at), (parts,), jnp.float32, smallest / len(shards), top_value / len(shards)))
        loudness = loudness * jnp.repeat(draws, dims[axis_at] // parts).reshape([-1 if axis == axis_at else 1 for axis in range(len(dims))])
    return loudness


def normal_values(stream_key, extent, scale, most, pieces=(), held_as=jnp.bfloat16):
    level = block_scale(stream_key, extent, pieces, -0.22, 0.18) if pieces else 1.0
    array = jax.random.normal(stream_key, extent, jnp.float32) * scale * level
    return jnp.minimum(jnp.maximum(array, -most), most).astype(held_as)


def setup_inputs(seed: int = 0) -> dict:
    arg_keys = jax.random.split(jax.random.key(seed), 13)
    return {
        "control": normal_values(arg_keys[0], (2, FIELDS, LEV, MM, MM), 1.0, 6.0, ((3, 256),), jnp.float32),
        "vertical": normal_values(arg_keys[1], (FIELDS, LEV, LEV, MM), LEV ** -0.5, 4.0, (), jnp.float32),
        "legendre": normal_values(arg_keys[2], (MM, MM, NHALF), (2 * MM * MM) ** -0.5, 0.0034179688, ((0, 256),)),
        "order_assign": jax.random.permutation(arg_keys[3], MM).astype(jnp.int32),
        "send_list": set_ends(jax.random.randint(arg_keys[4], (N_ORDER, N_LAT, N_LAT * CAP), 0, BLOCKS_DEV), jax.random.fold_in(arg_keys[4], 1), 0, BLOCKS_DEV - 1).astype(jnp.int32),
        "used_slot_counts": draw_used_slot_counts(jax.random.fold_in(arg_keys[12], 71), 0),
        "obs_count": set_ends(jax.random.randint(arg_keys[6], (N_ORDER, N_LAT, N_LAT * CAP), 1, KOBS + 1), jax.random.fold_in(arg_keys[6], 1), 1, KOBS).astype(jnp.int32),
        "obs_var": set_ends(jax.random.randint(arg_keys[7], (N_ORDER, N_LAT, OBSERVATION_SLOTS), 0, VARS), jax.random.fold_in(arg_keys[7], 1), 0, VARS - 1).astype(jnp.int32),
        "obs_col": set_ends(jax.random.randint(arg_keys[8], (N_ORDER, N_LAT, OBSERVATION_SLOTS), 0, BLKW - 3), jax.random.fold_in(arg_keys[8], 1), 0, (BLKW - 3) - 1).astype(jnp.int32),
        "obs_weight": jnp.clip(0.1 + 0.79999997 * jax.random.uniform(arg_keys[9], (4, N_ORDER, N_LAT, OBSERVATION_SLOTS), jnp.float32) ** block_scale(arg_keys[9], (4, N_ORDER, N_LAT, OBSERVATION_SLOTS), ((1, 8), (2, 32)), -0.2, 0.2), 0.1, 0.9),
        "obs_value": normal_values(arg_keys[10], (N_ORDER, N_LAT, OBSERVATION_SLOTS), 1.0, 6.0, ((0, 8), (1, 32)), jnp.float32),
        "obs_error": jnp.clip(jnp.exp(math.log(1.0) - 2.3025851 * jax.random.uniform(arg_keys[11], (N_ORDER, N_LAT, OBSERVATION_SLOTS), jnp.float32) ** block_scale(arg_keys[11], (N_ORDER, N_LAT, OBSERVATION_SLOTS), ((0, 8), (1, 32)), -0.2, 0.2)), 0.1, 1.0),
    }


def phase_rows(orders, lon_total):
    longitudes = lax.iota(jnp.int32, lon_total)
    turn_index = (orders.astype(jnp.int32)[:, None] * longitudes[None, :]) % lon_total
    angles = turn_index.astype(jnp.float32) * jnp.float32(2.0 * math.pi / lon_total)
    weight = jnp.where(orders == 0, 1.0, 2.0).astype(jnp.float32)[:, None]
    return jnp.stack([weight * jnp.cos(angles), -(weight * jnp.sin(angles))]).astype(jnp.bfloat16)


def vertical_mix(lookup, coeffs):
    summed = lookup[None, :, :, 0] * coeffs[:, :, None, 0]
    for level_index in range(1, coeffs.shape[2]):
        summed = summed + lookup[None, :, :, level_index] * coeffs[:, :, None, level_index]
    return summed


def vertical_back(lookup, incoming):
    summed = lookup[None, :, 0] * incoming[:, :, 0][:, :, None]
    for level_index in range(1, incoming.shape[2]):
        summed = summed + lookup[None, :, level_index] * incoming[:, :, level_index][:, :, None]
    return summed


def synthesis(coeffs, legendre_rows):
    var_count = coeffs.shape[1]
    order_count = coeffs.shape[2]
    deg_count = coeffs.shape[3]
    half_rows = legendre_rows.shape[2]
    coeff_pairs = coeffs.astype(jnp.float32).reshape(2, var_count, order_count, deg_count // 2, 2)
    table_rows = legendre_rows.astype(jnp.float32).reshape(order_count, deg_count // 2, 2, half_rows)
    parities = jnp.einsum("cvmhp,mhpk->pmcvk", coeff_pairs, table_rows, precision=lax.Precision.HIGHEST)
    northern = parities[0] + parities[1]
    southern = jnp.flip(parities[0] - parities[1], axis=3)
    return jnp.concatenate([northern, southern], axis=3).astype(jnp.bfloat16)


def analysis(incoming, legendre_rows):
    half_rows = legendre_rows.shape[2]
    table_rows = legendre_rows.astype(jnp.float32)
    northern = incoming[..., :half_rows].astype(jnp.float32)
    southern = jnp.flip(incoming[..., half_rows:], axis=3).astype(jnp.float32)
    from_north = jnp.einsum("mcvk,mjk->cvmj", northern, table_rows, precision=lax.Precision.HIGHEST)
    from_south = jnp.einsum("mcvk,mjk->cvmj", southern, table_rows, precision=lax.Precision.HIGHEST)
    alternate = jnp.where(lax.iota(jnp.int32, table_rows.shape[1]) % 2 == 0, 1.0, -1.0).astype(jnp.float32)
    return from_north + alternate * from_south


def interpolate(flat_values, positions, weights):
    seen_values = weights[0] * jnp.take(flat_values, positions).astype(jnp.float32)
    for offset in range(1, 4):
        seen_values = seen_values + weights[offset] * jnp.take(flat_values, positions + offset).astype(jnp.float32)
    return seen_values


def spread(positions, weights, weighted, total_size):
    summed = jnp.zeros((total_size,), jnp.float32)
    for offset in range(4):
        summed = summed.at[positions + offset].add(weights[offset] * weighted)
    return summed


def reference(control, vertical, legendre, order_assign, send_list, used_slot_counts, obs_count, obs_var, obs_col, obs_weight, obs_value, obs_error):
    field_count = control.shape[1]
    level_count = control.shape[2]
    order_total = control.shape[3]
    var_count = field_count * level_count
    lat_total = 2 * legendre.shape[2]
    lon_total = NLON
    group_size = math.gcd(order_total, 64)
    group_total = order_total // group_size

    def block_setup(block_index):
        first_slot = (block_index * group_size).astype(jnp.int32)
        orders = lax.dynamic_slice_in_dim(order_assign, first_slot, group_size)
        degrees = orders[:, None] + lax.iota(jnp.int32, order_total)[None, :]
        is_live = degrees < order_total
        lookup = jnp.take(vertical, jnp.minimum(degrees, order_total - 1), axis=3)
        coeffs = lax.dynamic_slice_in_dim(control, first_slot, group_size, 3)
        table_rows = lax.dynamic_slice_in_dim(legendre, first_slot, group_size, 0)
        return is_live, lookup, coeffs, table_rows

    def forward_block(block_index):
        is_live, lookup, coeffs, table_rows = block_setup(block_index)
        mixed_coeffs = jnp.where(is_live, vertical_mix(lookup, coeffs), 0.0)
        mixed_coeffs = mixed_coeffs.reshape(2, var_count, group_size, order_total).astype(jnp.bfloat16)
        return synthesis(mixed_coeffs, table_rows)

    block_ids = jnp.arange(group_total, dtype=jnp.int32)
    fourier = lax.map(forward_block, block_ids).reshape(order_total, 2, var_count, lat_total)
    phases = phase_rows(order_assign, lon_total).astype(jnp.float32)
    increment = jnp.einsum("icvr,cil->rvl", fourier.astype(jnp.float32), phases, precision=lax.Precision.HIGHEST).astype(jnp.bfloat16)

    rows_dev = lat_total // (N_ORDER * N_LAT)
    lon_blocks = lon_total // BLKW
    block_count = rows_dev * lon_blocks
    width = var_count * BLKW
    blocks = increment.reshape(N_ORDER, N_LAT, rows_dev, var_count, lon_blocks, BLKW).transpose(0, 1, 2, 4, 3, 5).reshape(-1)
    obs_shape = obs_value.shape
    owner_order = lax.broadcasted_iota(jnp.int32, obs_shape, 0)
    owner_lat = lax.broadcasted_iota(jnp.int32, obs_shape, 1)
    obs_index = lax.broadcasted_iota(jnp.int32, obs_shape, 2)
    slot_index = obs_index // KOBS
    source = slot_index // CAP
    slot_in = slot_index % CAP
    within = obs_index % KOBS
    chosen = jnp.take(send_list.reshape(-1), ((owner_order * N_LAT + source) * N_LAT + owner_lat) * CAP + slot_in)
    slot_live = slot_in < jnp.take(used_slot_counts.reshape(-1), (owner_order * N_LAT + owner_lat) * N_LAT + source)
    obs_live = within < jnp.take(obs_count.reshape(-1), (owner_order * N_LAT + owner_lat) * (N_LAT * CAP) + slot_index)
    is_seen = (slot_live & obs_live).reshape(-1)
    positions = (((owner_order * N_LAT + source) * block_count + chosen) * width + obs_var * BLKW + obs_col).reshape(-1)
    weights = obs_weight.reshape(4, -1)
    seen_values = interpolate(blocks, positions, weights)
    weighted = jnp.where(is_seen, (seen_values - obs_value.reshape(-1)) / obs_error.reshape(-1), 0.0)
    back_grads = spread(positions, weights, weighted, blocks.shape[0])
    grid_grad = back_grads.reshape(N_ORDER, N_LAT, rows_dev, lon_blocks, var_count, BLKW).transpose(0, 1, 2, 4, 3, 5)
    grid_grad = grid_grad.reshape(lat_total, var_count, lon_total).astype(jnp.bfloat16)
    fourier_grad = jnp.einsum("rvl,cil->icvr", grid_grad.astype(jnp.float32), phases, precision=lax.Precision.HIGHEST).astype(jnp.bfloat16)

    def backward_block(block_index):
        is_live, lookup, coeffs, table_rows = block_setup(block_index)
        incoming = lax.dynamic_slice_in_dim(fourier_grad, (block_index * group_size).astype(jnp.int32), group_size, 0)
        spectral = analysis(incoming, table_rows).reshape(2, field_count, level_count, group_size, order_total)
        return coeffs + jnp.where(is_live, vertical_back(lookup, spectral), 0.0)

    gradient = lax.map(backward_block, block_ids)
    gradient = jnp.moveaxis(gradient, 0, 3).reshape(2, field_count, level_count, order_total, order_total)
    return increment, weighted.reshape(obs_shape), gradient
```

```python
import functools
import math

import jax
import jax.numpy as jnp
from jax import lax
from jax.experimental import pallas as pl
from jax.experimental.pallas import tpu as pltpu
from jax.sharding import PartitionSpec as P

NLON = 2560
QUARTER = NLON // 4
BLKW = 64
CAP = 8
KOBS = 16
MM = 1280
NHALF = 640
VARS = 6
ROWS = 5
ORDERS = 5
DEVS = 256
N_LAT = 32
CHUNKS = NLON // 128
F32 = jnp.float32
BF16 = jnp.bfloat16
NT = (((1,), (1,)), ((), ()))


def lanes(shape, axis):
    return lax.broadcasted_iota(jnp.int32, shape, axis)


def pack_obs(var_ref, col_ref, weight_ref, value_ref, error_ref, used_ref, count_ref, out_ref):
    source = lanes((N_LAT, DEVS), 0)
    slot = lanes((N_LAT, DEVS), 1)
    mine = jnp.where(slot // CAP == source, count_ref[...].astype(F32), 0.0).astype(BF16)
    spread = (lanes((DEVS, 128), 0) % CAP == lanes((DEVS, 128), 1) // KOBS).astype(F32).astype(BF16)
    counts = jnp.dot(mine, spread, preferred_element_type=F32)
    own = lanes((N_LAT, N_LAT), 0) == lanes((N_LAT, N_LAT), 1)
    used = jnp.sum(jnp.where(own, used_ref[...].astype(F32), 0.0), axis=1, keepdims=True)
    lane = lanes((N_LAT, 128), 1)
    live = ((lane // KOBS).astype(F32) < used) & ((lane % KOBS).astype(F32) < counts)
    fields = [weight_ref[w] for w in range(4)]
    fields.append(var_ref[...].astype(F32))
    fields.append(col_ref[...].astype(F32))
    fields.append(value_ref[...])
    fields.append(jnp.where(live, 1.0 / error_ref[...], 0.0))
    for index, field in enumerate(fields):
        out_ref[pl.ds(index, N_LAT, stride=8), :] = field


def row_picks(half, row):
    device = lanes((128, NHALF), 0)
    at = lanes((128, NHALF), 1)
    want = device * ROWS + row if half == 0 else (NHALF - 1 - row) - device * ROWS
    return jnp.where(at == want, 1.0, 0.0).astype(BF16)


def start_tables(legendre_ref, table_ref, sems):
    copies = [
        pltpu.make_async_copy(legendre_ref.at[i], table_ref.at[i], sems.at[i]) for i in range(ORDERS)
    ]
    for copy in copies:
        copy.start()
    return copies


def alternate_signs():
    return jnp.where(lanes((1, MM), 1) % 2 == 0, 1.0, -1.0)


def synth_kernel(
    order_ref, vertical_ref, control_ref, legendre_ref, out_ref, lookup_ref, table_ref, padded_ref, mixed_ref, half_ref, rows_ref, sems
):
    copies = start_tables(legendre_ref, table_ref, sems)
    first = (lax.axis_index("order") * N_LAT + lax.axis_index("lat")) * ORDERS
    padded_ref[...] = jnp.zeros_like(padded_ref)
    for f in range(3):
        for a in range(2):
            padded_ref[pl.ds(f * 4 + a * 2, 2), pl.ds(0, MM)] = vertical_ref[f, a]
    for i in range(ORDERS):
        order = order_ref[first + i]
        base = pl.multiple_of((order // 128) * 128, 128)
        window = padded_ref[:, pl.ds(base, MM + 128)]
        window = pltpu.roll(window, (MM + 128) - order % 128, 1)
        for u in range(MM // 128):
            lookup_ref[u, pl.ds(i, 12, stride=8), :] = window[:12, 128 * u : 128 * u + 128]
    for c in range(2):
        for f in range(3):
            for a in range(2):
                for u in range(MM // 128):
                    at = pl.ds(128 * u, 128)
                    mix = lookup_ref[u, pl.ds((f * 4 + a * 2) * 8, ORDERS), :] * control_ref[c * 6 + f * 2, :, at]
                    other = lookup_ref[u, pl.ds((f * 4 + a * 2 + 1) * 8, ORDERS), :]
                    mix = mix + other * control_ref[c * 6 + f * 2 + 1, :, at]
                    mixed_ref[u, pl.ds((c * 6 + f * 2 + a) * 8, ORDERS), :] = mix
    signs = alternate_signs()
    half_ref[...] = jnp.zeros_like(half_ref)
    for i in range(ORDERS):
        coeffs = jnp.concatenate([mixed_ref[u, pl.ds(i, 12, stride=8), :] for u in range(MM // 128)], axis=1)
        signed = jnp.concatenate([coeffs, coeffs * signs], axis=0).astype(BF16)
        copies[i].wait()
        both = jnp.dot(signed, table_ref[i], preferred_element_type=F32)
        half_ref[0, pl.ds(12 * i, 12), :] = both[:12]
        half_ref[1, pl.ds(12 * i, 12), :] = both[12:]
    low = lanes((128, 128), 1) < 64
    for half in range(2):
        rows = half_ref[half].astype(BF16)
        rows = jnp.concatenate([rows, rows], axis=0)
        picked = [
            lax.dot_general(row_picks(half, j), rows, NT, preferred_element_type=F32) for j in range(ROWS)
        ]
        picked.append(jnp.zeros_like(picked[0]))
        for jj in range(3):
            rows_ref[pl.ds(half * 512 + jj, 128, stride=4), :] = jnp.where(low, picked[2 * jj], picked[2 * jj + 1])
        rows_ref[pl.ds(half * 512 + 3, 128, stride=4), :] = jnp.zeros((128, 128), F32)
    out_ref[...] = rows_ref[...].astype(BF16)


def turn(steps):
    quadrant = jnp.floor(steps * (1.0 / QUARTER) + 0.5)
    angle = (steps - quadrant * QUARTER) * (2.0 * math.pi / NLON)
    square = angle * angle
    sine = angle * (
        1.0 + square * (-1.0 / 6 + square * (1.0 / 120 + square * (-1.0 / 5040 + square * (1.0 / 362880))))
    )
    cosine = 1.0 + square * (
        -0.5 + square * (1.0 / 24 + square * (-1.0 / 720 + square * (1.0 / 40320 - square * (1.0 / 3628800))))
    )
    part = quadrant - 4.0 * jnp.floor(quadrant * 0.25)
    odd = (part == 1.0) | (part == 3.0)
    cos_sign = jnp.where((part == 1.0) | (part == 2.0), -1.0, 1.0)
    sin_sign = jnp.where(part >= 2.0, -1.0, 1.0)
    return cos_sign * jnp.where(odd, sine, cosine), sin_sign * jnp.where(odd, cosine, sine)


def phase_kernel(order_ref, out_ref):
    lane = lanes((DEVS, 128), 1).astype(F32)
    for i in range(ORDERS):
        order = order_ref[:, i : i + 1].astype(F32)
        weight = jnp.where(order == 0.0, 1.0, 2.0)
        fine_cos, fine_sin = turn(order * lane)
        fine_cos, fine_sin = fine_cos * weight, fine_sin * weight
        for a in range(QUARTER // 128):
            big_cos, big_sin = turn(order * (128.0 * a))
            out_ref[pl.ds(i * DEVS, DEVS), pl.ds(128 * a, 128)] = (fine_cos * big_cos - fine_sin * big_sin).astype(BF16)
            out_ref[pl.ds((ORDERS + i) * DEVS, DEVS), pl.ds(128 * a, 128)] = (
                -(fine_sin * big_cos + fine_cos * big_sin)
            ).astype(BF16)


def class_masks(order_row):
    residue = order_row % 4
    zero = jnp.where(residue == 0, 1.0, 0.0)
    two = jnp.where(residue == 2, 1.0, 0.0)
    odd = jnp.where(residue % 2 == 1, 1.0, 0.0)
    turned = jnp.where(residue == 1, 1.0, jnp.where(residue == 3, -1.0, 0.0))
    return zero, two, odd, turned


def middle_kernel(
    send_smem, send_ref, order_ref, obs_ref, rows_ref, phase_ref, inc_ref, out_ref,
    wide_ref, turned_ref, grouped_ref, lhs_ref, grid_ref, acc_ref, seen_ref,
):
    wide_ref[...] = rows_ref[...].astype(F32)
    for jj in range(3):
        turned_ref[pl.ds(128 * jj, 128), :] = wide_ref[pl.ds(jj, DEVS, stride=4), :].T
    grouped_ref[...] = jnp.zeros_like(grouped_ref)
    for g in range(2 * ORDERS):
        for j in range(ROWS):
            grouped_ref[g, pl.ds(6 * j, 6), :] = turned_ref[pl.ds(64 * j + 6 * g, 6), :]
    masks = [class_masks(order_ref[i : i + 1, :]) for i in range(ORDERS)]
    for i in range(ORDERS):
        zero, two, odd, turned = masks[i]
        real, imag = grouped_ref[2 * i], grouped_ref[2 * i + 1]
        by_cos = jnp.concatenate([real * zero, real * two, real * odd, imag * turned], axis=0)
        by_sin = jnp.concatenate([imag * zero, imag * two, imag * odd, -(real * turned)], axis=0)
        lhs_ref[:, pl.ds(i * DEVS, DEVS)] = by_cos.astype(BF16)
        lhs_ref[:, pl.ds((ORDERS + i) * DEVS, DEVS)] = by_sin.astype(BF16)
    sums = jnp.dot(lhs_ref[...], phase_ref[...], preferred_element_type=F32)
    r0, r2, ro, io = (sums[32 * k : 32 * k + 32] for k in range(4))
    even, skew = r0 + r2, r0 - r2
    quarters = [even + ro, skew - io, even - ro, skew + io]
    for a in range(4):
        rounded = quarters[a].astype(BF16).astype(F32)
        for u in range(5):
            grid_ref[a * 5 + u] = rounded[:, 128 * u : 128 * u + 128]
        for j in range(ROWS):
            inc_ref[j, :, pl.ds(QUARTER * a, QUARTER)] = rounded[6 * j : 6 * j + 6].astype(BF16)
    acc_ref[...] = jnp.zeros_like(acc_ref)
    source = lanes((N_LAT, DEVS), 0)
    slot = lanes((N_LAT, DEVS), 1)
    mine = jnp.where(slot // CAP == source, send_ref[...] % 2, 0).astype(F32).astype(BF16)
    spread = (lanes((DEVS, 128), 0) % CAP == lanes((DEVS, 128), 1) // KOBS).astype(F32).astype(BF16)
    seen_ref[...] = jnp.dot(mine, spread, preferred_element_type=F32) * BLKW
    across = lanes((128, 128), 0).astype(F32)
    pair_code = lanes((64, 128), 0).astype(F32)
    slot_code = (lanes((1, 128), 1) // KOBS * 8).astype(F32)

    def observe(d):
        fields = [obs_ref[pl.ds(d * 8 + f, 1), :] for f in range(8)]
        places, tiles = [], []
        for t in range(CAP):
            block = jnp.clip(send_smem[d * CAP + t], 0, 199)
            j = (block * 1639) >> 16
            places.append(((block - 40 * j) >> 1, 6 * j))
            tiles.append(grid_ref[places[t][0], pl.ds(places[t][1], 8), :])
        blocks = jnp.concatenate(tiles, axis=0)
        offset = across - (fields[5] + seen_ref[pl.ds(d, 1), :])
        table = jnp.where(offset == 3.0, fields[3], 0.0)
        for w in (2, 1, 0):
            table = jnp.where(offset == float(w), fields[w], table)
        hot = jnp.where(pair_code == fields[4] + slot_code, 1.0, 0.0).astype(BF16)
        picks = jnp.dot(blocks.T.astype(BF16), hot, preferred_element_type=F32)
        seen = jnp.sum(picks * table, axis=0, keepdims=True)
        weighted = (seen - fields[6]) * fields[7]
        seen_ref[pl.ds(d, 1), :] = weighted
        back = table * weighted
        high = back.astype(BF16)
        rest = (back - high.astype(F32)).astype(BF16)
        spreads = lax.dot_general(hot, high, NT, preferred_element_type=F32) + lax.dot_general(
            hot, rest, NT, preferred_element_type=F32
        )
        for t in range(CAP):
            chunk, row = places[t]
            acc_ref[chunk, pl.ds(row, 8), :] += spreads[8 * t : 8 * t + 8]

    def observe_group(k, carry):
        for d in range(4):
            observe(k * 4 + d)
        return carry

    lax.fori_loop(0, N_LAT // 4, observe_group, 0)
    grads = [
        jnp.concatenate([acc_ref[a * 5 + u] for u in range(5)], axis=1).astype(BF16).astype(F32) for a in range(4)
    ]
    even, other = grads[0] + grads[2], grads[1] + grads[3]
    folded = jnp.concatenate([even + other, even - other, grads[0] - grads[2], grads[1] - grads[3]], axis=0)
    back = lax.dot_general(folded.astype(BF16), phase_ref[...], NT, preferred_element_type=F32)
    for i in range(ORDERS):
        zero, two, odd, turned = masks[i]
        by_cos = back[:, i * DEVS : (i + 1) * DEVS]
        by_sin = back[:, (ORDERS + i) * DEVS : (ORDERS + i + 1) * DEVS]
        grouped_ref[2 * i] = by_cos[:32] * zero + by_cos[32:64] * two + by_cos[64:96] * odd + by_sin[96:] * turned
        grouped_ref[2 * i + 1] = by_sin[:32] * zero + by_sin[32:64] * two + by_sin[64:96] * odd - by_cos[96:] * turned
    for g in range(2 * ORDERS):
        for j in range(ROWS):
            turned_ref[pl.ds(64 * j + 6 * g, 6), :] = grouped_ref[g, pl.ds(6 * j, 6), :]
    for jj in range(3):
        wide_ref[pl.ds(jj, DEVS, stride=4), :] = turned_ref[pl.ds(128 * jj, 128), :].T
    for o in range(DEVS // N_LAT):
        wide_ref[pl.ds(4 * N_LAT * o + 3, N_LAT, stride=4), :] = seen_ref[...]
    out_ref[...] = wide_ref[...].astype(BF16)


def analysis_kernel(
    rows_ref, lookup_ref, control_ref, legendre_ref, weighted_ref, grad_ref, table_ref, wide_ref, turned_ref, half_ref, spectral_ref, sems
):
    copies = start_tables(legendre_ref, table_ref, sems)
    wide_ref[...] = rows_ref[...].astype(F32)
    first = lax.axis_index("order") * (4 * N_LAT)
    weighted_ref[...] = wide_ref[pl.ds(first + 3, N_LAT, stride=4), :]
    for jj in range(3):
        turned_ref[pl.ds(128 * jj, 128), :] = wide_ref[pl.ds(jj, DEVS, stride=4), :].T
    for half in range(2):
        total = jnp.zeros((64, NHALF), F32)
        for j in range(ROWS):
            piece = turned_ref[pl.ds(64 * j, 64), pl.ds(128 * half, 128)].astype(BF16)
            total = total + jnp.dot(piece, row_picks(half, j), preferred_element_type=F32)
        half_ref[half] = total
    signs = alternate_signs()
    for i in range(ORDERS):
        both = jnp.concatenate(
            [half_ref[0, pl.ds(12 * i, 12), :], half_ref[1, pl.ds(12 * i, 12), :]], axis=0
        ).astype(BF16)
        copies[i].wait()
        sums = lax.dot_general(both, table_ref[i], NT, preferred_element_type=F32)
        sums = sums[:12] + signs * sums[12:]
        for u in range(MM // 128):
            spectral_ref[u, pl.ds(i, 12, stride=8), :] = sums[:, 128 * u : 128 * u + 128]
    for c in range(2):
        for f in range(3):
            for b in range(2):
                for u in range(MM // 128):
                    at = pl.ds(128 * u, 128)
                    total = control_ref[c * 6 + f * 2 + b, :, at]
                    for a in range(2):
                        factor = lookup_ref[u, pl.ds((f * 4 + a * 2 + b) * 8, ORDERS), :]
                        total = total + factor * spectral_ref[u, pl.ds((c * 6 + f * 2 + a) * 8, ORDERS), :]
                    grad_ref[c * 6 + f * 2 + b, :, at] = total


VMEM = pl.BlockSpec(memory_space=pltpu.VMEM)
SMEM = pl.BlockSpec(memory_space=pltpu.SMEM)
HBM = pl.BlockSpec(memory_space=pl.ANY)


def grant(mib):
    return pltpu.CompilerParams(vmem_limit_bytes=mib * 1024 * 1024)


def shards(
    control, vertical, legendre, order_assign, send_list, used_slot_counts, obs_count, obs_var, obs_col, obs_weight, obs_value, obs_error
):
    shape = jax.ShapeDtypeStruct
    with jax.named_scope("pack_obs"):
        packed = pl.pallas_call(
            pack_obs, out_shape=shape((DEVS, 128), F32), in_specs=[VMEM] * 7, out_specs=VMEM, name="pack_obs",
        )(
            obs_var.reshape(N_LAT, 128), obs_col.reshape(N_LAT, 128), obs_weight.reshape(4, N_LAT, 128),
            obs_value.reshape(N_LAT, 128), obs_error.reshape(N_LAT, 128),
            used_slot_counts.reshape(1, N_LAT), obs_count.reshape(1, DEVS),
        )
    obs = lax.all_to_all(packed.reshape(N_LAT, 8, 128), "lat", split_axis=0, concat_axis=0, tiled=True)
    coeffs = control.reshape(12, ORDERS, MM)
    with jax.named_scope("synthesis"):
        outgoing, lookup = pl.pallas_call(
            synth_kernel,
            out_shape=(shape((4 * DEVS, 128), BF16), shape((MM // 128, 96, 128), F32)),
            in_specs=[SMEM, VMEM, VMEM, HBM],
            out_specs=(VMEM, VMEM),
            scratch_shapes=[
                pltpu.VMEM((ORDERS, MM, NHALF), BF16),
                pltpu.VMEM((16, 2 * MM + 128), F32),
                pltpu.VMEM((MM // 128, 96, 128), F32),
                pltpu.VMEM((2, 64, NHALF), F32),
                pltpu.VMEM((4 * DEVS, 128), F32),
                pltpu.SemaphoreType.DMA((ORDERS,)),
            ],
            compiler_params=grant(28),
            cost_estimate=pl.CostEstimate(flops=2 * 24 * 5 * MM * NHALF, bytes_accessed=9 << 20, transcendentals=0),
            name="synthesis",
        )(order_assign, vertical, coeffs, legendre)
    arrived = lax.all_to_all(
        outgoing.reshape(DEVS, 4, 128), ("order", "lat"), split_axis=0, concat_axis=0, tiled=True
    ).reshape(4 * DEVS, 128)
    by_device = order_assign.reshape(DEVS, ORDERS)
    with jax.named_scope("phases"):
        phases = pl.pallas_call(
            phase_kernel,
            out_shape=shape((2 * ORDERS * DEVS, QUARTER), BF16),
            in_specs=[VMEM],
            out_specs=VMEM,
            compiler_params=grant(16),
            cost_estimate=pl.CostEstimate(flops=40_000_000, bytes_accessed=4 << 20, transcendentals=0),
            name="phases",
        )(by_device)
    with jax.named_scope("middle"):
        increment, returning = pl.pallas_call(
            middle_kernel,
            out_shape=(shape((ROWS, VARS, NLON), BF16), shape((4 * DEVS, 128), BF16)),
            in_specs=[SMEM, VMEM, VMEM, VMEM, VMEM, VMEM],
            out_specs=(VMEM, VMEM),
            scratch_shapes=[
                pltpu.VMEM((4 * DEVS, 128), F32),
                pltpu.VMEM((384, DEVS), F32),
                pltpu.VMEM((2 * ORDERS, 32, DEVS), F32),
                pltpu.VMEM((128, 2 * ORDERS * DEVS), BF16),
                pltpu.VMEM((CHUNKS, 32, 128), F32),
                pltpu.VMEM((CHUNKS, 32, 128), F32),
                pltpu.VMEM((N_LAT, 128), F32),
            ],
            compiler_params=grant(28),
            name="middle",
        )(send_list.reshape(DEVS), send_list.reshape(1, DEVS), by_device.T, obs.reshape(DEVS, 128), arrived, phases)
    returned = lax.all_to_all(
        returning.reshape(DEVS, 4, 128), ("order", "lat"), split_axis=0, concat_axis=0, tiled=True
    ).reshape(4 * DEVS, 128)
    with jax.named_scope("analysis"):
        weighted, gradient = pl.pallas_call(
            analysis_kernel,
            out_shape=(shape((N_LAT, 128), F32), shape((12, ORDERS, MM), F32)),
            in_specs=[VMEM, VMEM, VMEM, HBM],
            out_specs=(VMEM, VMEM),
            scratch_shapes=[
                pltpu.VMEM((ORDERS, MM, NHALF), BF16),
                pltpu.VMEM((4 * DEVS, 128), F32),
                pltpu.VMEM((384, DEVS), F32),
                pltpu.VMEM((2, 64, NHALF), F32),
                pltpu.VMEM((MM // 128, 96, 128), F32),
                pltpu.SemaphoreType.DMA((ORDERS,)),
            ],
            compiler_params=grant(28),
            name="analysis",
        )(returned, lookup, coeffs, legendre)
    return increment, weighted.reshape(obs_value.shape), gradient.reshape(control.shape)


def solution(mesh):
    return jax.shard_map(
        shards,
        mesh=mesh,
        in_specs=(
            P(None, None, None, ("order", "lat"), None),
            P(),
            P(("order", "lat"), None, None),
            P(),
            P("order", "lat", None),
            P("order", "lat", None),
            P("order", "lat", None),
            P("order", "lat", None),
            P("order", "lat", None),
            P(None, "order", "lat", None),
            P("order", "lat", None),
            P("order", "lat", None),
        ),
        out_specs=(
            P(("order", "lat"), None, None),
            P("order", "lat", None),
            P(None, None, None, ("order", "lat"), None),
        ),
        check_vma=False,
    )
```

```python
import functools
import math

import jax
import jax.numpy as jnp
from jax import lax
from jax.experimental import pallas as pl
from jax.experimental.pallas import tpu as pltpu
from jax.sharding import PartitionSpec as P

NLON = 2560
QUARTER = NLON // 4
BLKW = 64
CAP = 8
KOBS = 16
MM = 1280
NHALF = 640
VARS = 6
ROWS = 5
ORDERS = 5
DEVS = 256
GROUP = 32
N_LAT = 32
CHUNKS = NLON // 128
F32 = jnp.float32
BF16 = jnp.bfloat16
NT = (((1,), (1,)), ((), ()))


def lanes(shape, axis):
    return lax.broadcasted_iota(jnp.int32, shape, axis)


def pack_obs(var_ref, col_ref, weight_ref, value_ref, error_ref, used_ref, count_ref, send_ref, out_ref, place_ref):
    block = jnp.clip(send_ref[...], 0, 199)
    row = (block * 1639) >> 16
    place_ref[...] = (block - 40 * row) * 32 + row * 6
    source = lanes((N_LAT, DEVS), 0)
    slot = lanes((N_LAT, DEVS), 1)
    mine = jnp.where(slot // CAP == source, count_ref[...].astype(F32), 0.0).astype(BF16)
    spread = (lanes((DEVS, 128), 0) % CAP == lanes((DEVS, 128), 1) // KOBS).astype(F32).astype(BF16)
    counts = jnp.dot(mine, spread, preferred_element_type=F32)
    own = lanes((N_LAT, N_LAT), 0) == lanes((N_LAT, N_LAT), 1)
    used = jnp.sum(jnp.where(own, used_ref[...].astype(F32), 0.0), axis=1, keepdims=True)
    lane = lanes((N_LAT, 128), 1)
    live = ((lane // KOBS).astype(F32) < used) & ((lane % KOBS).astype(F32) < counts)
    fields = [weight_ref[w] for w in range(4)]
    fields.append(var_ref[...].astype(F32))
    fields.append(col_ref[...].astype(F32))
    fields.append(value_ref[...])
    fields.append(jnp.where(live, 1.0 / error_ref[...], 0.0))
    for index, field in enumerate(fields):
        out_ref[pl.ds(index, N_LAT, stride=8), :] = field


def row_picks(half, row):
    device = lanes((128, NHALF), 0)
    at = lanes((128, NHALF), 1)
    want = device * ROWS + row if half == 0 else (NHALF - 1 - row) - device * ROWS
    return jnp.where(at == want, 1.0, 0.0).astype(BF16)


def alternate_signs():
    return jnp.where(lanes((1, MM), 1) % 2 == 0, 1.0, -1.0)


def start_tables(legendre_ref, table_ref, sems):
    copies = [pltpu.make_async_copy(legendre_ref.at[i], table_ref.at[i], sems.at[i]) for i in range(ORDERS)]
    for copy in copies:
        copy.start(priority=1)
    return copies


def start_small(order_ref, vertical_ref, control_ref, order_smem, vertical_buf, control_buf, sems):
    copies = [
        pltpu.make_async_copy(order_ref, order_smem, sems.at[0]),
        pltpu.make_async_copy(vertical_ref, vertical_buf, sems.at[1]),
        pltpu.make_async_copy(control_ref, control_buf, sems.at[2]),
    ]
    for copy in copies:
        copy.start()
    return copies


def pad_vertical(vertical_buf, padded_ref):
    padded_ref[...] = jnp.zeros_like(padded_ref)
    for f in range(3):
        for a in range(2):
            padded_ref[pl.ds(f * 4 + a * 2, 2), pl.ds(0, MM)] = vertical_buf[f, a]


def lookup_rows(order, padded_ref):
    base = pl.multiple_of((order // 128) * 128, 128)
    window = padded_ref[:, pl.ds(base, MM + 128)]
    return pltpu.roll(window, (MM + 128) - order % 128, 1)[:, :MM]


def first_slot():
    return (lax.axis_index("order") * N_LAT + lax.axis_index("lat")) * ORDERS


def synth_kernel(
    order_ref, vertical_ref, control_ref, legendre_ref, out_ref,
    order_smem, vertical_buf, control_buf, table_ref, padded_ref, mixed_ref, half_ref, rows_ref, small_sems, sems,
):
    small = start_small(order_ref, vertical_ref, control_ref, order_smem, vertical_buf, control_buf, small_sems)
    copies = start_tables(legendre_ref, table_ref, sems)
    half_ref[...] = jnp.zeros_like(half_ref)
    for copy in small:
        copy.wait()
    pad_vertical(vertical_buf, padded_ref)
    signs = alternate_signs()
    for i in range(ORDERS):
        lookup = lookup_rows(order_smem[first_slot() + i], padded_ref)
        rows = []
        for c in range(2):
            for f in range(3):
                coeffs = control_buf[c, f, i]
                for a in range(2):
                    at = f * 4 + a * 2
                    rows.append(jnp.sum(lookup[at : at + 2] * coeffs, axis=0, keepdims=True))
        coeffs = jnp.concatenate(rows, axis=0)
        mixed_ref[i] = jnp.concatenate([coeffs, coeffs * signs], axis=0).astype(BF16)
    for i in range(ORDERS):
        copies[i].wait()
        both = jnp.dot(mixed_ref[i], table_ref[i], preferred_element_type=F32)
        half_ref[0, pl.ds(12 * i, 12), :] = both[:12]
        half_ref[1, pl.ds(12 * i, 12), :] = both[12:]
    low = lanes((128, 128), 1) < 64
    for half in range(2):
        rows = half_ref[half].astype(BF16)
        rows = jnp.concatenate([rows, rows], axis=0)
        picked = [
            lax.dot_general(row_picks(half, j), rows, NT, preferred_element_type=F32) for j in range(ROWS)
        ]
        picked.append(jnp.zeros_like(picked[0]))
        for jj in range(3):
            rows_ref[pl.ds(half * 512 + jj, 128, stride=4), :] = jnp.where(low, picked[2 * jj], picked[2 * jj + 1])
        rows_ref[pl.ds(half * 512 + 3, 128, stride=4), :] = jnp.zeros((128, 128), F32)
    out_ref[...] = rows_ref[...].astype(BF16)


def turn(steps):
    quadrant = jnp.floor(steps * (1.0 / QUARTER) + 0.5)
    angle = (steps - quadrant * QUARTER) * (2.0 * math.pi / NLON)
    square = angle * angle
    sine = angle * (
        1.0 + square * (-1.0 / 6 + square * (1.0 / 120 + square * (-1.0 / 5040 + square * (1.0 / 362880))))
    )
    cosine = 1.0 + square * (
        -0.5 + square * (1.0 / 24 + square * (-1.0 / 720 + square * (1.0 / 40320 - square * (1.0 / 3628800))))
    )
    part = quadrant - 4.0 * jnp.floor(quadrant * 0.25)
    odd = (part == 1.0) | (part == 3.0)
    cos_sign = jnp.where((part == 1.0) | (part == 2.0), -1.0, 1.0)
    sin_sign = jnp.where(part >= 2.0, -1.0, 1.0)
    return cos_sign * jnp.where(odd, sine, cosine), sin_sign * jnp.where(odd, cosine, sine)


def phase_kernel(order_ref, out_ref):
    lane = lanes((DEVS, 128), 1).astype(F32)
    for i in range(ORDERS):
        order = order_ref[:, i : i + 1].astype(F32)
        weight = jnp.where(order == 0.0, 1.0, 2.0)
        fine_cos, fine_sin = turn(order * lane)
        fine_cos, fine_sin = fine_cos * weight, fine_sin * weight
        for a in range(QUARTER // 128):
            big_cos, big_sin = turn(order * (128.0 * a))
            out_ref[pl.ds(i * DEVS, DEVS), pl.ds(128 * a, 128)] = (fine_cos * big_cos - fine_sin * big_sin).astype(BF16)
            out_ref[pl.ds((ORDERS + i) * DEVS, DEVS), pl.ds(128 * a, 128)] = (
                -(fine_sin * big_cos + fine_cos * big_sin)
            ).astype(BF16)


def class_masks(order_row):
    residue = order_row % 4
    zero = jnp.where(residue == 0, 1.0, 0.0)
    two = jnp.where(residue == 2, 1.0, 0.0)
    odd = jnp.where(residue % 2 == 1, 1.0, 0.0)
    turned = jnp.where(residue == 1, 1.0, jnp.where(residue == 3, -1.0, 0.0))
    return zero, two, odd, turned


def middle_kernel(
    place_smem, order_ref, obs_ref, rows_ref, phase_ref, inc_ref, out_ref,
    wide_ref, turned_ref, grouped_ref, lhs_ref, grid_ref, acc_ref, seen_ref, table_ref, hot_ref,
):
    wide_ref[...] = rows_ref[...].astype(F32)
    for jj in range(3):
        turned_ref[pl.ds(128 * jj, 128), :] = wide_ref[pl.ds(jj, DEVS, stride=4), :].T
    grouped_ref[...] = jnp.zeros_like(grouped_ref)
    for g in range(2 * ORDERS):
        for j in range(ROWS):
            grouped_ref[g, pl.ds(6 * j, 6), :] = turned_ref[pl.ds(64 * j + 6 * g, 6), :]
    masks = [class_masks(order_ref[i : i + 1, :]) for i in range(ORDERS)]
    for i in range(ORDERS):
        zero, two, odd, turned = masks[i]
        real, imag = grouped_ref[2 * i], grouped_ref[2 * i + 1]
        by_cos = jnp.concatenate([real * zero, real * two, real * odd, imag * turned], axis=0)
        by_sin = jnp.concatenate([imag * zero, imag * two, imag * odd, -(real * turned)], axis=0)
        lhs_ref[:, pl.ds(i * DEVS, DEVS)] = by_cos.astype(BF16)
        lhs_ref[:, pl.ds((ORDERS + i) * DEVS, DEVS)] = by_sin.astype(BF16)
    sums = jnp.dot(lhs_ref[...], phase_ref[...], preferred_element_type=F32)
    r0, r2, ro, io = (sums[32 * k : 32 * k + 32] for k in range(4))
    even, skew = r0 + r2, r0 - r2
    quarters = [even + ro, skew - io, even - ro, skew + io]
    for a in range(4):
        rounded = quarters[a].astype(BF16).astype(F32)
        for u in range(5):
            pair = rounded[:, 128 * u : 128 * u + 128]
            grid_ref[pl.ds((a * 5 + u) * 64, 32), :] = pair
            grid_ref[pl.ds((a * 5 + u) * 64 + 32, 32), :] = pltpu.roll(pair, BLKW, 1)
        for j in range(ROWS):
            inc_ref[j, :, pl.ds(QUARTER * a, QUARTER)] = rounded[6 * j : 6 * j + 6].astype(BF16)
    acc_ref[...] = jnp.zeros_like(acc_ref)
    across = lanes((BLKW, 128), 0).astype(F32)
    pair_code = lanes((64, 128), 0).astype(F32)
    slot_code = (lanes((1, 128), 1) // KOBS * 8).astype(F32)

    def look(d):
        fields = [obs_ref[pl.ds(d * 8 + f, 1), :] for f in range(6)]
        tiles = [grid_ref[pl.ds(place_smem[d * CAP + t], 8), :] for t in range(CAP)]
        offset = across - fields[5]
        table = jnp.where(offset == 3.0, fields[3], 0.0)
        for w in (2, 1, 0):
            table = jnp.where(offset == float(w), fields[w], table)
        hot = jnp.where(pair_code == fields[4] + slot_code, 1.0, 0.0).astype(BF16)
        blocks = jnp.concatenate(tiles, axis=0).T[:BLKW].astype(BF16)
        picks = jnp.dot(blocks, hot, preferred_element_type=F32)
        table_ref[d] = table
        hot_ref[d] = hot
        seen_ref[pl.ds(d, 1), :] = jnp.sum(picks * table, axis=0, keepdims=True)

    def add_back(d):
        back = (table_ref[d] * seen_ref[pl.ds(d, 1), :]).astype(BF16)
        spreads = lax.dot_general(hot_ref[d], back, NT, preferred_element_type=F32)
        for t in range(CAP):
            acc_ref[pl.ds(place_smem[d * CAP + t], 8), pl.ds(0, BLKW)] += spreads[8 * t : 8 * t + 8]

    def in_groups(step):
        def group(k, carry):
            for d in range(GROUP):
                step(k * GROUP + d)
            return carry

        lax.fori_loop(0, N_LAT // GROUP, group, 0)

    in_groups(look)
    values = obs_ref[pl.ds(6, N_LAT, stride=8), :]
    scales = obs_ref[pl.ds(7, N_LAT, stride=8), :]
    seen_ref[...] = (seen_ref[...] - values) * scales
    in_groups(add_back)
    low = lanes((32, 128), 1) < BLKW

    def pair_of(u):
        return jnp.where(low, acc_ref[pl.ds(u * 64, 32), :], pltpu.roll(acc_ref[pl.ds(u * 64 + 32, 32), :], BLKW, 1))

    grads = [
        jnp.concatenate([pair_of(a * 5 + u) for u in range(5)], axis=1).astype(BF16).astype(F32) for a in range(4)
    ]
    even, other = grads[0] + grads[2], grads[1] + grads[3]
    folded = jnp.concatenate([even + other, even - other, grads[0] - grads[2], grads[1] - grads[3]], axis=0)
    back = lax.dot_general(folded.astype(BF16), phase_ref[...], NT, preferred_element_type=F32)
    for i in range(ORDERS):
        zero, two, odd, turned = masks[i]
        by_cos = back[:, i * DEVS : (i + 1) * DEVS]
        by_sin = back[:, (ORDERS + i) * DEVS : (ORDERS + i + 1) * DEVS]
        grouped_ref[2 * i] = by_cos[:32] * zero + by_cos[32:64] * two + by_cos[64:96] * odd + by_sin[96:] * turned
        grouped_ref[2 * i + 1] = by_sin[:32] * zero + by_sin[32:64] * two + by_sin[64:96] * odd - by_cos[96:] * turned
    for g in range(2 * ORDERS):
        for j in range(ROWS):
            turned_ref[pl.ds(64 * j + 6 * g, 6), :] = grouped_ref[g, pl.ds(6 * j, 6), :]
    for jj in range(3):
        wide_ref[pl.ds(jj, DEVS, stride=4), :] = turned_ref[pl.ds(128 * jj, 128), :].T
    for o in range(DEVS // N_LAT):
        wide_ref[pl.ds(4 * N_LAT * o + 3, N_LAT, stride=4), :] = seen_ref[...]
    out_ref[...] = wide_ref[...].astype(BF16)


def analysis_kernel(
    order_ref, vertical_ref, control_ref, legendre_ref, rows_ref, weighted_ref, grad_ref,
    order_smem, vertical_buf, control_buf, table_ref, padded_ref, lookup_ref, wide_ref, turned_ref, half_ref, grad_buf,
    small_sems, sems, out_sems,
):
    small = start_small(order_ref, vertical_ref, control_ref, order_smem, vertical_buf, control_buf, small_sems)
    copies = start_tables(legendre_ref, table_ref, sems)
    wide_ref[...] = rows_ref[...].astype(F32)
    first = lax.axis_index("order") * (4 * N_LAT)
    weighted_ref[...] = wide_ref[pl.ds(first + 3, N_LAT, stride=4), :]
    for jj in range(3):
        turned_ref[pl.ds(128 * jj, 128), :] = wide_ref[pl.ds(jj, DEVS, stride=4), :].T
    for half in range(2):
        total = jnp.zeros((64, NHALF), F32)
        for j in range(ROWS):
            piece = turned_ref[pl.ds(64 * j, 64), pl.ds(128 * half, 128)].astype(BF16)
            total = total + jnp.dot(piece, row_picks(half, j), preferred_element_type=F32)
        half_ref[half] = total
    for copy in small:
        copy.wait()
    pad_vertical(vertical_buf, padded_ref)
    for i in range(ORDERS):
        lookup_ref[i] = lookup_rows(order_smem[first_slot() + i], padded_ref)
    signs = alternate_signs()
    outs = []
    for i in range(ORDERS):
        both = jnp.concatenate(
            [half_ref[0, pl.ds(12 * i, 12), :], half_ref[1, pl.ds(12 * i, 12), :]], axis=0
        ).astype(BF16)
        copies[i].wait()
        sums = lax.dot_general(both, table_ref[i], NT, preferred_element_type=F32)
        spectral = sums[:12] + signs * sums[12:]
        for c in range(2):
            for f in range(3):
                total = control_buf[c, f, i]
                for a in range(2):
                    at = c * 6 + f * 2 + a
                    total = total + lookup_ref[i, pl.ds(f * 4 + a * 2, 2), :] * spectral[at : at + 1]
                grad_buf[i, c, f] = total
        outs.append(pltpu.make_async_copy(grad_buf.at[i], grad_ref.at[:, :, i], out_sems.at[i]))
        outs[i].start()
    for out in outs:
        out.wait()


VMEM = pl.BlockSpec(memory_space=pltpu.VMEM)
SMEM = pl.BlockSpec(memory_space=pltpu.SMEM)
HBM = pl.BlockSpec(memory_space=pl.ANY)


def grant(mib):
    return pltpu.CompilerParams(vmem_limit_bytes=mib * 1024 * 1024)


def shards(
    control, vertical, legendre, order_assign, send_list, used_slot_counts, obs_count, obs_var, obs_col, obs_weight, obs_value, obs_error
):
    shape = jax.ShapeDtypeStruct
    with jax.named_scope("pack_obs"):
        packed, places = pl.pallas_call(
            pack_obs,
            out_shape=(shape((DEVS, 128), F32), shape((1, DEVS), jnp.int32)),
            in_specs=[VMEM] * 8,
            out_specs=(VMEM, VMEM),
            name="pack_obs",
        )(
            obs_var.reshape(N_LAT, 128), obs_col.reshape(N_LAT, 128), obs_weight.reshape(4, N_LAT, 128),
            obs_value.reshape(N_LAT, 128), obs_error.reshape(N_LAT, 128),
            used_slot_counts.reshape(1, N_LAT), obs_count.reshape(1, DEVS), send_list.reshape(1, DEVS),
        )
    obs = lax.all_to_all(packed.reshape(N_LAT, 8, 128), "lat", split_axis=0, concat_axis=0, tiled=True)
    coeffs = control.transpose(0, 1, 3, 2, 4)
    small_scratch = [
        pltpu.SMEM((MM,), jnp.int32),
        pltpu.VMEM(vertical.shape, F32),
        pltpu.VMEM(coeffs.shape, F32),
        pltpu.VMEM((ORDERS, MM, NHALF), BF16),
        pltpu.VMEM((16, 2 * MM + 128), F32),
    ]
    with jax.named_scope("synthesis"):
        outgoing = pl.pallas_call(
            synth_kernel,
            out_shape=shape((4 * DEVS, 128), BF16),
            in_specs=[HBM] * 4,
            out_specs=VMEM,
            scratch_shapes=small_scratch
            + [
                pltpu.VMEM((ORDERS, 24, MM), BF16),
                pltpu.VMEM((2, 64, NHALF), F32),
                pltpu.VMEM((4 * DEVS, 128), F32),
                pltpu.SemaphoreType.DMA((3,)),
                pltpu.SemaphoreType.DMA((ORDERS,)),
            ],
            compiler_params=grant(60),
            cost_estimate=pl.CostEstimate(flops=2 * 24 * 5 * MM * NHALF, bytes_accessed=9 << 20, transcendentals=0),
            name="synthesis",
        )(order_assign, vertical, coeffs, legendre)
    arrived = lax.all_to_all(
        outgoing.reshape(DEVS, 4, 128), ("order", "lat"), split_axis=0, concat_axis=0, tiled=True
    ).reshape(4 * DEVS, 128)
    by_device = order_assign.reshape(DEVS, ORDERS)
    with jax.named_scope("phases"):
        phases = pl.pallas_call(
            phase_kernel,
            out_shape=shape((2 * ORDERS * DEVS, QUARTER), BF16),
            in_specs=[VMEM],
            out_specs=VMEM,
            compiler_params=grant(16),
            cost_estimate=pl.CostEstimate(flops=40_000_000, bytes_accessed=4 << 20, transcendentals=0),
            name="phases",
        )(by_device)
    with jax.named_scope("middle"):
        increment, returning = pl.pallas_call(
            middle_kernel,
            out_shape=(shape((ROWS, VARS, NLON), BF16), shape((4 * DEVS, 128), BF16)),
            in_specs=[SMEM, VMEM, VMEM, VMEM, VMEM],
            out_specs=(VMEM, VMEM),
            scratch_shapes=[
                pltpu.VMEM((4 * DEVS, 128), F32),
                pltpu.VMEM((384, DEVS), F32),
                pltpu.VMEM((2 * ORDERS, 32, DEVS), F32),
                pltpu.VMEM((128, 2 * ORDERS * DEVS), BF16),
                pltpu.VMEM((2 * CHUNKS * 32, 128), F32),
                pltpu.VMEM((2 * CHUNKS * 32, 128), F32),
                pltpu.VMEM((N_LAT, 128), F32),
                pltpu.VMEM((N_LAT, BLKW, 128), F32),
                pltpu.VMEM((N_LAT, 64, 128), BF16),
            ],
            compiler_params=grant(28),
            name="middle",
        )(places.reshape(DEVS), by_device.T, obs.reshape(DEVS, 128), arrived, phases)
    returned = lax.all_to_all(
        returning.reshape(DEVS, 4, 128), ("order", "lat"), split_axis=0, concat_axis=0, tiled=True
    ).reshape(4 * DEVS, 128)
    with jax.named_scope("analysis"):
        weighted, gradient = pl.pallas_call(
            analysis_kernel,
            out_shape=(shape((N_LAT, 128), F32), shape(coeffs.shape, F32)),
            in_specs=[HBM] * 4 + [VMEM],
            out_specs=(VMEM, HBM),
            scratch_shapes=small_scratch
            + [
                pltpu.VMEM((ORDERS, 16, MM), F32),
                pltpu.VMEM((4 * DEVS, 128), F32),
                pltpu.VMEM((384, DEVS), F32),
                pltpu.VMEM((2, 64, NHALF), F32),
                pltpu.VMEM((ORDERS, 2, 3, 2, MM), F32),
                pltpu.SemaphoreType.DMA((3,)),
                pltpu.SemaphoreType.DMA((ORDERS,)),
                pltpu.SemaphoreType.DMA((ORDERS,)),
            ],
            compiler_params=grant(60),
            name="analysis",
        )(order_assign, vertical, coeffs, legendre, returned)
    return increment, weighted.reshape(obs_value.shape), gradient.transpose(0, 1, 3, 2, 4)


def solution(mesh):
    return jax.shard_map(
        shards,
        mesh=mesh,
        in_specs=(
            P(None, None, None, ("order", "lat"), None),
            P(),
            P(("order", "lat"), None, None),
            P(),
            P("order", "lat", None),
            P("order", "lat", None),
            P("order", "lat", None),
            P("order", "lat", None),
            P("order", "lat", None),
            P(None, "order", "lat", None),
            P("order", "lat", None),
            P("order", "lat", None),
        ),
        out_specs=(
            P(("order", "lat"), None, None),
            P("order", "lat", None),
            P(None, None, None, ("order", "lat"), None),
        ),
        check_vma=False,
    )
```

```python
import functools
import math

import jax
import jax.numpy as jnp
from jax import lax
from jax.experimental import pallas as pl
from jax.experimental.pallas import tpu as pltpu
from jax.sharding import PartitionSpec as P

NLON = 2560
QUARTER = NLON // 4
BLKW = 64
CAP = 8
KOBS = 16
MM = 1280
NHALF = 640
VARS = 6
ROWS = 5
ORDERS = 5
DEVS = 256
GROUP = 32
N_LAT = 32
CHUNKS = NLON // 128
F32 = jnp.float32
BF16 = jnp.bfloat16
NT = (((1,), (1,)), ((), ()))


def lanes(shape, axis):
    return lax.broadcasted_iota(jnp.int32, shape, axis)


def pack_obs(var_ref, col_ref, weight_ref, value_ref, error_ref, used_ref, count_ref, send_ref, out_ref, place_ref):
    block = jnp.clip(send_ref[...], 0, 199)
    row = (block * 1639) >> 16
    place_ref[...] = (block - 40 * row) * 32 + row * 6
    source = lanes((N_LAT, DEVS), 0)
    slot = lanes((N_LAT, DEVS), 1)
    mine = jnp.where(slot // CAP == source, count_ref[...].astype(F32), 0.0).astype(BF16)
    spread = (lanes((DEVS, 128), 0) % CAP == lanes((DEVS, 128), 1) // KOBS).astype(F32).astype(BF16)
    counts = jnp.dot(mine, spread, preferred_element_type=F32)
    own = lanes((N_LAT, N_LAT), 0) == lanes((N_LAT, N_LAT), 1)
    used = jnp.sum(jnp.where(own, used_ref[...].astype(F32), 0.0), axis=1, keepdims=True)
    lane = lanes((N_LAT, 128), 1)
    live = ((lane // KOBS).astype(F32) < used) & ((lane % KOBS).astype(F32) < counts)
    fields = [weight_ref[w] for w in range(4)]
    fields.append(var_ref[...].astype(F32))
    fields.append(col_ref[...].astype(F32))
    fields.append(value_ref[...])
    fields.append(jnp.where(live, 1.0 / error_ref[...], 0.0))
    for index, field in enumerate(fields):
        out_ref[pl.ds(index, N_LAT, stride=8), :] = field


def row_picks(half, row):
    device = lanes((128, NHALF), 0)
    at = lanes((128, NHALF), 1)
    want = device * ROWS + row if half == 0 else (NHALF - 1 - row) - device * ROWS
    return jnp.where(at == want, 1.0, 0.0).astype(BF16)


def alternate_signs():
    return jnp.where(lanes((1, MM), 1) % 2 == 0, 1.0, -1.0)


def start_tables(legendre_ref, table_ref, sems):
    copies = [pltpu.make_async_copy(legendre_ref.at[i], table_ref.at[i], sems.at[i]) for i in range(ORDERS)]
    for copy in copies:
        copy.start(priority=1)
    return copies


def start_small(order_ref, vertical_ref, control_ref, order_smem, vertical_buf, control_buf, sems):
    copies = [
        pltpu.make_async_copy(order_ref, order_smem, sems.at[0]),
        pltpu.make_async_copy(vertical_ref, vertical_buf, sems.at[1]),
        pltpu.make_async_copy(control_ref, control_buf, sems.at[2]),
    ]
    for copy in copies:
        copy.start()
    return copies


def pad_vertical(vertical_buf, padded_ref):
    padded_ref[...] = jnp.zeros_like(padded_ref)
    for f in range(3):
        for a in range(2):
            padded_ref[pl.ds(f * 4 + a * 2, 2), pl.ds(0, MM)] = vertical_buf[f, a]


def lookup_rows(order, padded_ref):
    base = pl.multiple_of((order // 128) * 128, 128)
    window = padded_ref[:, pl.ds(base, MM + 128)]
    return pltpu.roll(window, (MM + 128) - order % 128, 1)[:, :MM]


def first_slot():
    return (lax.axis_index("order") * N_LAT + lax.axis_index("lat")) * ORDERS


def synth_kernel(
    order_ref, vertical_ref, control_ref, legendre_ref, out_ref,
    order_smem, vertical_buf, control_buf, table_ref, padded_ref, mixed_ref, half_ref, rows_ref, small_sems, sems,
):
    small = start_small(order_ref, vertical_ref, control_ref, order_smem, vertical_buf, control_buf, small_sems)
    copies = start_tables(legendre_ref, table_ref, sems)
    half_ref[...] = jnp.zeros_like(half_ref)
    for copy in small:
        copy.wait()
    pad_vertical(vertical_buf, padded_ref)
    signs = alternate_signs()
    for i in range(ORDERS):
        lookup = lookup_rows(order_smem[first_slot() + i], padded_ref)
        rows = []
        for c in range(2):
            for f in range(3):
                coeffs = control_buf[c, f, i]
                for a in range(2):
                    at = f * 4 + a * 2
                    rows.append(jnp.sum(lookup[at : at + 2] * coeffs, axis=0, keepdims=True))
        coeffs = jnp.concatenate(rows, axis=0)
        mixed_ref[i] = jnp.concatenate([coeffs, coeffs * signs], axis=0).astype(BF16)
    for i in range(ORDERS):
        copies[i].wait()
        both = jnp.dot(mixed_ref[i], table_ref[i], preferred_element_type=F32)
        half_ref[0, pl.ds(12 * i, 12), :] = both[:12]
        half_ref[1, pl.ds(12 * i, 12), :] = both[12:]
    low = lanes((128, 128), 1) < 64
    for half in range(2):
        rows = half_ref[half].astype(BF16)
        rows = jnp.concatenate([rows, rows], axis=0)
        picked = [
            lax.dot_general(row_picks(half, j), rows, NT, preferred_element_type=F32) for j in range(ROWS)
        ]
        picked.append(jnp.zeros_like(picked[0]))
        for jj in range(3):
            rows_ref[pl.ds(half * 512 + jj, 128, stride=4), :] = jnp.where(low, picked[2 * jj], picked[2 * jj + 1])
        rows_ref[pl.ds(half * 512 + 3, 128, stride=4), :] = jnp.zeros((128, 128), F32)
    out_ref[...] = rows_ref[...].astype(BF16)


def turn(steps):
    quadrant = jnp.floor(steps * (1.0 / QUARTER) + 0.5)
    angle = (steps - quadrant * QUARTER) * (2.0 * math.pi / NLON)
    square = angle * angle
    sine = angle * (
        1.0 + square * (-1.0 / 6 + square * (1.0 / 120 + square * (-1.0 / 5040 + square * (1.0 / 362880))))
    )
    cosine = 1.0 + square * (
        -0.5 + square * (1.0 / 24 + square * (-1.0 / 720 + square * (1.0 / 40320 - square * (1.0 / 3628800))))
    )
    part = quadrant - 4.0 * jnp.floor(quadrant * 0.25)
    odd = (part == 1.0) | (part == 3.0)
    cos_sign = jnp.where((part == 1.0) | (part == 2.0), -1.0, 1.0)
    sin_sign = jnp.where(part >= 2.0, -1.0, 1.0)
    return cos_sign * jnp.where(odd, sine, cosine), sin_sign * jnp.where(odd, cosine, sine)


def phase_kernel(order_ref, out_ref):
    lane = lanes((DEVS, 128), 1)
    coarse = jnp.zeros((DEVS, 128), F32)
    orders = [order_ref[:, i : i + 1].astype(F32) for i in range(ORDERS)]
    for i in range(ORDERS):
        coarse = jnp.where(lane // 5 == i, orders[i], coarse)
    weight = jnp.where(coarse == 0.0, 1.0, 2.0)
    coarse_cos, coarse_sin = turn(coarse * (128 * (lane % 5)).astype(F32))
    coarse_cos, coarse_sin = coarse_cos * weight, coarse_sin * weight
    lane = lane.astype(F32)
    for i in range(ORDERS):
        fine_cos, fine_sin = turn(orders[i] * lane)
        for a in range(QUARTER // 128):
            at = i * 5 + a
            big_cos, big_sin = coarse_cos[:, at : at + 1], coarse_sin[:, at : at + 1]
            out_ref[pl.ds(i * DEVS, DEVS), pl.ds(128 * a, 128)] = (fine_cos * big_cos - fine_sin * big_sin).astype(BF16)
            out_ref[pl.ds((ORDERS + i) * DEVS, DEVS), pl.ds(128 * a, 128)] = (
                -(fine_sin * big_cos + fine_cos * big_sin)
            ).astype(BF16)


def class_masks(order_row):
    residue = order_row % 4
    zero = jnp.where(residue == 0, 1.0, 0.0)
    two = jnp.where(residue == 2, 1.0, 0.0)
    odd = jnp.where(residue % 2 == 1, 1.0, 0.0)
    turned = jnp.where(residue == 1, 1.0, jnp.where(residue == 3, -1.0, 0.0))
    return zero, two, odd, turned


def middle_kernel(
    place_smem, order_ref, obs_ref, rows_ref, phase_ref, inc_ref, out_ref,
    wide_ref, turned_ref, grouped_ref, lhs_ref, grid_ref, acc_ref, seen_ref, table_ref, hot_ref,
):
    wide_ref[...] = rows_ref[...].astype(F32)
    for jj in range(3):
        turned_ref[pl.ds(128 * jj, 128), :] = wide_ref[pl.ds(jj, DEVS, stride=4), :].T
    grouped_ref[...] = jnp.zeros_like(grouped_ref)
    for g in range(2 * ORDERS):
        for j in range(ROWS):
            grouped_ref[g, pl.ds(6 * j, 6), :] = turned_ref[pl.ds(64 * j + 6 * g, 6), :]
    masks = [class_masks(order_ref[i : i + 1, :]) for i in range(ORDERS)]
    for i in range(ORDERS):
        zero, two, odd, turned = masks[i]
        real, imag = grouped_ref[2 * i], grouped_ref[2 * i + 1]
        by_cos = jnp.concatenate([real * zero, real * two, real * odd, imag * turned], axis=0)
        by_sin = jnp.concatenate([imag * zero, imag * two, imag * odd, -(real * turned)], axis=0)
        lhs_ref[:, pl.ds(i * DEVS, DEVS)] = by_cos.astype(BF16)
        lhs_ref[:, pl.ds((ORDERS + i) * DEVS, DEVS)] = by_sin.astype(BF16)
    sums = jnp.dot(lhs_ref[...], phase_ref[...], preferred_element_type=F32)
    r0, r2, ro, io = (sums[32 * k : 32 * k + 32] for k in range(4))
    even, skew = r0 + r2, r0 - r2
    quarters = [even + ro, skew - io, even - ro, skew + io]
    for a in range(4):
        rounded = quarters[a].astype(BF16).astype(F32)
        for u in range(5):
            pair = rounded[:, 128 * u : 128 * u + 128]
            grid_ref[pl.ds((a * 5 + u) * 64, 32), :] = pair
            grid_ref[pl.ds((a * 5 + u) * 64 + 32, 32), :] = pltpu.roll(pair, BLKW, 1)
        for j in range(ROWS):
            inc_ref[j, :, pl.ds(QUARTER * a, QUARTER)] = rounded[6 * j : 6 * j + 6].astype(BF16)
    acc_ref[...] = jnp.zeros_like(acc_ref)
    across = lanes((BLKW, 128), 0).astype(F32)
    pair_code = lanes((64, 128), 0).astype(F32)
    slot_code = (lanes((1, 128), 1) // KOBS * 8).astype(F32)

    def look(d):
        fields = [obs_ref[pl.ds(d * 8 + f, 1), :] for f in range(6)]
        tiles = [grid_ref[pl.ds(place_smem[d * CAP + t], 8), :] for t in range(CAP)]
        offset = across - fields[5]
        table = jnp.where(offset == 3.0, fields[3], 0.0)
        for w in (2, 1, 0):
            table = jnp.where(offset == float(w), fields[w], table)
        hot = jnp.where(pair_code == fields[4] + slot_code, 1.0, 0.0).astype(BF16)
        blocks = jnp.concatenate(tiles, axis=0).T[:BLKW].astype(BF16)
        picks = jnp.dot(blocks, hot, preferred_element_type=F32)
        table_ref[d] = table
        hot_ref[d] = hot
        seen_ref[pl.ds(d, 1), :] = jnp.sum(picks * table, axis=0, keepdims=True)

    def add_back(d):
        back = (table_ref[d] * seen_ref[pl.ds(d, 1), :]).astype(BF16)
        spreads = lax.dot_general(hot_ref[d], back, NT, preferred_element_type=F32)
        for t in range(CAP):
            acc_ref[pl.ds(place_smem[d * CAP + t], 8), pl.ds(0, BLKW)] += spreads[8 * t : 8 * t + 8]

    def in_groups(step):
        def group(k, carry):
            for d in range(GROUP):
                step(k * GROUP + d)
            return carry

        lax.fori_loop(0, N_LAT // GROUP, group, 0)

    in_groups(look)
    values = obs_ref[pl.ds(6, N_LAT, stride=8), :]
    scales = obs_ref[pl.ds(7, N_LAT, stride=8), :]
    seen_ref[...] = (seen_ref[...] - values) * scales
    in_groups(add_back)
    low = lanes((32, 128), 1) < BLKW

    def pair_of(u):
        return jnp.where(low, acc_ref[pl.ds(u * 64, 32), :], pltpu.roll(acc_ref[pl.ds(u * 64 + 32, 32), :], BLKW, 1))

    grads = [
        jnp.concatenate([pair_of(a * 5 + u) for u in range(5)], axis=1).astype(BF16).astype(F32) for a in range(4)
    ]
    even, other = grads[0] + grads[2], grads[1] + grads[3]
    folded = jnp.concatenate([even + other, even - other, grads[0] - grads[2], grads[1] - grads[3]], axis=0)
    back = lax.dot_general(folded.astype(BF16), phase_ref[...], NT, preferred_element_type=F32)
    for i in range(ORDERS):
        zero, two, odd, turned = masks[i]
        by_cos = back[:, i * DEVS : (i + 1) * DEVS]
        by_sin = back[:, (ORDERS + i) * DEVS : (ORDERS + i + 1) * DEVS]
        grouped_ref[2 * i] = by_cos[:32] * zero + by_cos[32:64] * two + by_cos[64:96] * odd + by_sin[96:] * turned
        grouped_ref[2 * i + 1] = by_sin[:32] * zero + by_sin[32:64] * two + by_sin[64:96] * odd - by_cos[96:] * turned
    for g in range(2 * ORDERS):
        for j in range(ROWS):
            turned_ref[pl.ds(64 * j + 6 * g, 6), :] = grouped_ref[g, pl.ds(6 * j, 6), :]
    for jj in range(3):
        wide_ref[pl.ds(jj, DEVS, stride=4), :] = turned_ref[pl.ds(128 * jj, 128), :].T
    for o in range(DEVS // N_LAT):
        wide_ref[pl.ds(4 * N_LAT * o + 3, N_LAT, stride=4), :] = seen_ref[...]
    out_ref[...] = wide_ref[...].astype(BF16)


def analysis_kernel(
    order_ref, vertical_ref, control_ref, legendre_ref, rows_ref, weighted_ref, grad_ref,
    order_smem, vertical_buf, control_buf, table_ref, padded_ref, lookup_ref, coeffs_ref, wide_ref, turned_ref, half_ref, both_ref, small_sems, sems,
):
    small = start_small(order_ref, vertical_ref, control_ref, order_smem, vertical_buf, control_buf, small_sems)
    copies = start_tables(legendre_ref, table_ref, sems)
    wide_ref[...] = rows_ref[...].astype(F32)
    first = lax.axis_index("order") * (4 * N_LAT)
    weighted_ref[...] = wide_ref[pl.ds(first + 3, N_LAT, stride=4), :]
    for jj in range(3):
        turned_ref[pl.ds(128 * jj, 128), :] = wide_ref[pl.ds(jj, DEVS, stride=4), :].T
    for half in range(2):
        total = jnp.zeros((64, NHALF), F32)
        for j in range(ROWS):
            piece = turned_ref[pl.ds(64 * j, 64), pl.ds(128 * half, 128)].astype(BF16)
            total = total + jnp.dot(piece, row_picks(half, j), preferred_element_type=F32)
        half_ref[half] = total
    at = lanes((160, 64), 0)
    source = (at // 32) * 12 + (at % 16) // 2 * 2 + (at // 16) % 2
    twice = jnp.where((lanes((160, 64), 1) == source) & (at % 16 < 12), 1.0, 0.0).astype(BF16)
    for half in range(2):
        both_ref[half] = jnp.dot(twice, half_ref[half].astype(BF16), preferred_element_type=F32)
    for copy in small:
        copy.wait()
    padded_ref[...] = jnp.zeros_like(padded_ref)
    for a in range(2):
        for c in range(2):
            for f in range(3):
                padded_ref[pl.ds(16 * a + c * 6 + f * 2, 2), pl.ds(0, MM)] = vertical_buf[f, a]
    for i in range(ORDERS):
        lookup_ref[i] = lookup_rows(order_smem[first_slot() + i], padded_ref)
        for c in range(2):
            for f in range(3):
                coeffs_ref[i, pl.ds(c * 6 + f * 2, 2), :] = control_buf[c, f, i]
    signs = alternate_signs()
    for i in range(ORDERS):
        both = jnp.concatenate([both_ref[0, pl.ds(32 * i, 32), :], both_ref[1, pl.ds(32 * i, 32), :]], axis=0)
        copies[i].wait()
        sums = lax.dot_general(both.astype(BF16), table_ref[i], NT, preferred_element_type=F32)
        spectral = (sums[:32] + signs * sums[32:]) * lookup_ref[i]
        total = coeffs_ref[i] + (spectral[:16] + spectral[16:])
        for c in range(2):
            for f in range(3):
                at = c * 6 + f * 2
                grad_ref[c, f, i] = total[at : at + 2]


VMEM = pl.BlockSpec(memory_space=pltpu.VMEM)
SMEM = pl.BlockSpec(memory_space=pltpu.SMEM)
HBM = pl.BlockSpec(memory_space=pl.ANY)


def grant(mib):
    return pltpu.CompilerParams(vmem_limit_bytes=mib * 1024 * 1024)


def shards(
    control, vertical, legendre, order_assign, send_list, used_slot_counts, obs_count, obs_var, obs_col, obs_weight, obs_value, obs_error
):
    shape = jax.ShapeDtypeStruct
    with jax.named_scope("pack_obs"):
        packed, places = pl.pallas_call(
            pack_obs,
            out_shape=(shape((DEVS, 128), F32), shape((1, DEVS), jnp.int32)),
            in_specs=[VMEM] * 8,
            out_specs=(VMEM, VMEM),
            name="pack_obs",
        )(
            obs_var.reshape(N_LAT, 128), obs_col.reshape(N_LAT, 128), obs_weight.reshape(4, N_LAT, 128),
            obs_value.reshape(N_LAT, 128), obs_error.reshape(N_LAT, 128),
            used_slot_counts.reshape(1, N_LAT), obs_count.reshape(1, DEVS), send_list.reshape(1, DEVS),
        )
    obs = lax.all_to_all(packed.reshape(N_LAT, 8, 128), "lat", split_axis=0, concat_axis=0, tiled=True)
    coeffs = control.transpose(0, 1, 3, 2, 4)
    small_scratch = [
        pltpu.SMEM((MM,), jnp.int32),
        pltpu.VMEM(vertical.shape, F32),
        pltpu.VMEM(coeffs.shape, F32),
        pltpu.VMEM((ORDERS, MM, NHALF), BF16),
    ]
    with jax.named_scope("synthesis"):
        outgoing = pl.pallas_call(
            synth_kernel,
            out_shape=shape((4 * DEVS, 128), BF16),
            in_specs=[HBM] * 4,
            out_specs=VMEM,
            scratch_shapes=small_scratch
            + [
                pltpu.VMEM((16, 2 * MM + 128), F32),
                pltpu.VMEM((ORDERS, 24, MM), BF16),
                pltpu.VMEM((2, 64, NHALF), F32),
                pltpu.VMEM((4 * DEVS, 128), F32),
                pltpu.SemaphoreType.DMA((3,)),
                pltpu.SemaphoreType.DMA((ORDERS,)),
            ],
            compiler_params=grant(60),
            cost_estimate=pl.CostEstimate(flops=2 * 24 * 5 * MM * NHALF, bytes_accessed=9 << 20, transcendentals=0),
            name="synthesis",
        )(order_assign, vertical, coeffs, legendre)
    arrived = lax.all_to_all(
        outgoing.reshape(DEVS, 4, 128), ("order", "lat"), split_axis=0, concat_axis=0, tiled=True
    ).reshape(4 * DEVS, 128)
    by_device = order_assign.reshape(DEVS, ORDERS)
    with jax.named_scope("phases"):
        phases = pl.pallas_call(
            phase_kernel,
            out_shape=shape((2 * ORDERS * DEVS, QUARTER), BF16),
            in_specs=[VMEM],
            out_specs=VMEM,
            compiler_params=grant(16),
            cost_estimate=pl.CostEstimate(flops=40_000_000, bytes_accessed=4 << 20, transcendentals=0),
            name="phases",
        )(by_device)
    with jax.named_scope("middle"):
        increment, returning = pl.pallas_call(
            middle_kernel,
            out_shape=(shape((ROWS, VARS, NLON), BF16), shape((4 * DEVS, 128), BF16)),
            in_specs=[SMEM, VMEM, VMEM, VMEM, VMEM],
            out_specs=(VMEM, VMEM),
            scratch_shapes=[
                pltpu.VMEM((4 * DEVS, 128), F32),
                pltpu.VMEM((384, DEVS), F32),
                pltpu.VMEM((2 * ORDERS, 32, DEVS), F32),
                pltpu.VMEM((128, 2 * ORDERS * DEVS), BF16),
                pltpu.VMEM((2 * CHUNKS * 32, 128), F32),
                pltpu.VMEM((2 * CHUNKS * 32, 128), F32),
                pltpu.VMEM((N_LAT, 128), F32),
                pltpu.VMEM((N_LAT, BLKW, 128), F32),
                pltpu.VMEM((N_LAT, 64, 128), BF16),
            ],
            compiler_params=grant(28),
            name="middle",
        )(places.reshape(DEVS), by_device.T, obs.reshape(DEVS, 128), arrived, phases)
    returned = lax.all_to_all(
        returning.reshape(DEVS, 4, 128), ("order", "lat"), split_axis=0, concat_axis=0, tiled=True
    ).reshape(4 * DEVS, 128)
    with jax.named_scope("analysis"):
        weighted, gradient = pl.pallas_call(
            analysis_kernel,
            out_shape=(shape((N_LAT, 128), F32), shape(coeffs.shape, F32)),
            in_specs=[HBM] * 4 + [VMEM],
            out_specs=(VMEM, VMEM),
            scratch_shapes=small_scratch
            + [
                pltpu.VMEM((32, 2 * MM + 128), F32),
                pltpu.VMEM((ORDERS, 32, MM), F32),
                pltpu.VMEM((ORDERS, 16, MM), F32),
                pltpu.VMEM((4 * DEVS, 128), F32),
                pltpu.VMEM((384, DEVS), F32),
                pltpu.VMEM((2, 64, NHALF), F32),
                pltpu.VMEM((2, 160, NHALF), F32),
                pltpu.SemaphoreType.DMA((3,)),
                pltpu.SemaphoreType.DMA((ORDERS,)),
            ],
            compiler_params=grant(60),
            name="analysis",
        )(order_assign, vertical, coeffs, legendre, returned)
    return increment, weighted.reshape(obs_value.shape), gradient.transpose(0, 1, 3, 2, 4)


def solution(mesh):
    return jax.shard_map(
        shards,
        mesh=mesh,
        in_specs=(
            P(None, None, None, ("order", "lat"), None),
            P(),
            P(("order", "lat"), None, None),
            P(),
            P("order", "lat", None),
            P("order", "lat", None),
            P("order", "lat", None),
            P("order", "lat", None),
            P("order", "lat", None),
            P(None, "order", "lat", None),
            P("order", "lat", None),
            P("order", "lat", None),
        ),
        out_specs=(
            P(("order", "lat"), None, None),
            P("order", "lat", None),
            P(None, None, None, ("order", "lat"), None),
        ),
        check_vma=False,
    )
```

```python
import functools
import math

import jax
import jax.numpy as jnp
from jax import lax
from jax.experimental import pallas as pl
from jax.experimental.pallas import tpu as pltpu
from jax.sharding import PartitionSpec as P

NLON = 2560
QUARTER = NLON // 4
BLKW = 64
CAP = 8
KOBS = 16
MM = 1280
NHALF = 640
VARS = 6
ROWS = 5
ORDERS = 5
DEVS = 256
GROUP = 32
N_LAT = 32
CHUNKS = NLON // 128
F32 = jnp.float32
BF16 = jnp.bfloat16
NT = (((1,), (1,)), ((), ()))


def lanes(shape, axis):
    return lax.broadcasted_iota(jnp.int32, shape, axis)


def pack_obs(var_ref, col_ref, weight_ref, value_ref, error_ref, used_ref, count_ref, send_ref, out_ref, place_ref):
    block = jnp.clip(send_ref[...], 0, 199)
    row = (block * 1639) >> 16
    place_ref[...] = (block - 40 * row) * 32 + row * 6
    source = lanes((N_LAT, DEVS), 0)
    slot = lanes((N_LAT, DEVS), 1)
    mine = jnp.where(slot // CAP == source, count_ref[...].astype(F32), 0.0).astype(BF16)
    spread = (lanes((DEVS, 128), 0) % CAP == lanes((DEVS, 128), 1) // KOBS).astype(F32).astype(BF16)
    counts = jnp.dot(mine, spread, preferred_element_type=F32)
    own = lanes((N_LAT, N_LAT), 0) == lanes((N_LAT, N_LAT), 1)
    used = jnp.sum(jnp.where(own, used_ref[...].astype(F32), 0.0), axis=1, keepdims=True)
    lane = lanes((N_LAT, 128), 1)
    live = ((lane // KOBS).astype(F32) < used) & ((lane % KOBS).astype(F32) < counts)
    fields = [weight_ref[w] for w in range(4)]
    fields.append(var_ref[...].astype(F32))
    fields.append(col_ref[...].astype(F32))
    fields.append(value_ref[...])
    fields.append(jnp.where(live, 1.0 / error_ref[...], 0.0))
    for index, field in enumerate(fields):
        out_ref[pl.ds(index, N_LAT, stride=8), :] = field


def row_picks(half, row):
    device = lanes((128, NHALF), 0)
    at = lanes((128, NHALF), 1)
    want = device * ROWS + row if half == 0 else (NHALF - 1 - row) - device * ROWS
    return jnp.where(at == want, 1.0, 0.0).astype(BF16)


def alternate_signs():
    return jnp.where(lanes((1, MM), 1) % 2 == 0, 1.0, -1.0)


def start_tables(legendre_ref, table_ref, sems):
    copies = [pltpu.make_async_copy(legendre_ref.at[i], table_ref.at[i], sems.at[i]) for i in range(ORDERS)]
    for copy in copies:
        copy.start(priority=1)
    return copies


def start_small(order_ref, vertical_ref, control_ref, order_smem, vertical_buf, control_buf, sems):
    copies = [
        pltpu.make_async_copy(order_ref, order_smem, sems.at[0]),
        pltpu.make_async_copy(vertical_ref, vertical_buf, sems.at[1]),
        pltpu.make_async_copy(control_ref, control_buf, sems.at[2]),
    ]
    for copy in copies:
        copy.start()
    return copies


def pad_vertical(vertical_buf, padded_ref):
    padded_ref[...] = jnp.zeros_like(padded_ref)
    for f in range(3):
        for a in range(2):
            padded_ref[pl.ds(f * 4 + a * 2, 2), pl.ds(0, MM)] = vertical_buf[f, a]


def lookup_rows(order, padded_ref):
    base = pl.multiple_of((order // 128) * 128, 128)
    window = padded_ref[:, pl.ds(base, MM + 128)]
    return pltpu.roll(window, (MM + 128) - order % 128, 1)[:, :MM]


def first_slot():
    return (lax.axis_index("order") * N_LAT + lax.axis_index("lat")) * ORDERS


def synth_kernel(
    order_ref, vertical_ref, control_ref, legendre_ref, out_ref,
    order_smem, vertical_buf, control_buf, table_ref, padded_ref, mixed_ref, half_ref, rows_ref, small_sems, sems,
):
    small = start_small(order_ref, vertical_ref, control_ref, order_smem, vertical_buf, control_buf, small_sems)
    copies = start_tables(legendre_ref, table_ref, sems)
    half_ref[...] = jnp.zeros_like(half_ref)
    for copy in small:
        copy.wait()
    pad_vertical(vertical_buf, padded_ref)
    signs = alternate_signs()
    for i in range(ORDERS):
        lookup = lookup_rows(order_smem[first_slot() + i], padded_ref)
        rows = []
        for c in range(2):
            for f in range(3):
                coeffs = control_buf[c, f, i]
                for a in range(2):
                    at = f * 4 + a * 2
                    rows.append(jnp.sum(lookup[at : at + 2] * coeffs, axis=0, keepdims=True))
        coeffs = jnp.concatenate(rows, axis=0)
        mixed_ref[i] = jnp.concatenate([coeffs, coeffs * signs], axis=0).astype(BF16)
    for i in range(ORDERS):
        copies[i].wait()
        both = jnp.dot(mixed_ref[i], table_ref[i], preferred_element_type=F32)
        half_ref[0, pl.ds(12 * i, 12), :] = both[:12]
        half_ref[1, pl.ds(12 * i, 12), :] = both[12:]
    low = lanes((128, 128), 1) < 64
    for half in range(2):
        rows = half_ref[half].astype(BF16)
        rows = jnp.concatenate([rows, rows], axis=0)
        picks = jnp.concatenate([row_picks(half, j) for j in range(ROWS)], axis=0)
        picked = lax.dot_general(picks, rows, NT, preferred_element_type=F32)
        picked = [picked[128 * j : 128 * j + 128] for j in range(ROWS)]
        picked.append(jnp.zeros_like(picked[0]))
        for jj in range(3):
            rows_ref[pl.ds(half * 512 + jj, 128, stride=4), :] = jnp.where(low, picked[2 * jj], picked[2 * jj + 1])
        rows_ref[pl.ds(half * 512 + 3, 128, stride=4), :] = jnp.zeros((128, 128), F32)
    out_ref[...] = rows_ref[...].astype(BF16)


def turn(steps):
    quadrant = jnp.floor(steps * (1.0 / QUARTER) + 0.5)
    angle = (steps - quadrant * QUARTER) * (2.0 * math.pi / NLON)
    square = angle * angle
    sine = angle * (
        1.0 + square * (-1.0 / 6 + square * (1.0 / 120 + square * (-1.0 / 5040 + square * (1.0 / 362880))))
    )
    cosine = 1.0 + square * (
        -0.5 + square * (1.0 / 24 + square * (-1.0 / 720 + square * (1.0 / 40320 - square * (1.0 / 3628800))))
    )
    part = quadrant - 4.0 * jnp.floor(quadrant * 0.25)
    odd = (part == 1.0) | (part == 3.0)
    cos_sign = jnp.where((part == 1.0) | (part == 2.0), -1.0, 1.0)
    sin_sign = jnp.where(part >= 2.0, -1.0, 1.0)
    return cos_sign * jnp.where(odd, sine, cosine), sin_sign * jnp.where(odd, cosine, sine)


def phase_kernel(order_ref, out_ref):
    lane = lanes((DEVS, 128), 1)
    coarse = jnp.zeros((DEVS, 128), F32)
    orders = [order_ref[:, i : i + 1].astype(F32) for i in range(ORDERS)]
    for i in range(ORDERS):
        coarse = jnp.where(lane // 5 == i, orders[i], coarse)
    weight = jnp.where(coarse == 0.0, 1.0, 2.0)
    coarse_cos, coarse_sin = turn(coarse * (128 * (lane % 5)).astype(F32))
    coarse_cos, coarse_sin = coarse_cos * weight, coarse_sin * weight
    lane = lane.astype(F32)
    for i in range(ORDERS):
        fine_cos, fine_sin = turn(orders[i] * lane)
        for a in range(QUARTER // 128):
            at = i * 5 + a
            big_cos, big_sin = coarse_cos[:, at : at + 1], coarse_sin[:, at : at + 1]
            out_ref[pl.ds(i * DEVS, DEVS), pl.ds(128 * a, 128)] = (fine_cos * big_cos - fine_sin * big_sin).astype(BF16)
            out_ref[pl.ds((ORDERS + i) * DEVS, DEVS), pl.ds(128 * a, 128)] = (
                -(fine_sin * big_cos + fine_cos * big_sin)
            ).astype(BF16)


def class_masks(order_row):
    residue = order_row % 4
    zero = jnp.where(residue == 0, 1.0, 0.0)
    two = jnp.where(residue == 2, 1.0, 0.0)
    odd = jnp.where(residue % 2 == 1, 1.0, 0.0)
    turned = jnp.where(residue == 1, 1.0, jnp.where(residue == 3, -1.0, 0.0))
    return zero, two, odd, turned


def middle_kernel(
    place_smem, order_ref, obs_ref, rows_ref, phase_ref, inc_ref, out_ref,
    wide_ref, turned_ref, grouped_ref, lhs_ref, grid_ref, acc_refs, seen_ref, table_ref, hot_ref, inc_buf, inc_sem,
):
    wide_ref[...] = rows_ref[...].astype(F32)
    for jj in range(3):
        turned_ref[pl.ds(128 * jj, 128), :] = wide_ref[pl.ds(jj, DEVS, stride=4), :].T
    grouped_ref[...] = jnp.zeros_like(grouped_ref)
    for g in range(2 * ORDERS):
        for j in range(ROWS):
            grouped_ref[g, pl.ds(6 * j, 6), :] = turned_ref[pl.ds(64 * j + 6 * g, 6), :]
    masks = [class_masks(order_ref[i : i + 1, :]) for i in range(ORDERS)]
    for i in range(ORDERS):
        zero, two, odd, turned = masks[i]
        real, imag = grouped_ref[2 * i], grouped_ref[2 * i + 1]
        by_cos = jnp.concatenate([real * zero, real * two, real * odd, imag * turned], axis=0)
        by_sin = jnp.concatenate([imag * zero, imag * two, imag * odd, -(real * turned)], axis=0)
        lhs_ref[:, pl.ds(i * DEVS, DEVS)] = by_cos.astype(BF16)
        lhs_ref[:, pl.ds((ORDERS + i) * DEVS, DEVS)] = by_sin.astype(BF16)
    sums = jnp.dot(lhs_ref[...], phase_ref[...], preferred_element_type=F32)
    r0, r2, ro, io = (sums[32 * k : 32 * k + 32] for k in range(4))
    even, skew = r0 + r2, r0 - r2
    quarters = [even + ro, skew - io, even - ro, skew + io]
    for a in range(4):
        rounded = quarters[a].astype(BF16).astype(F32)
        for u in range(5):
            pair = rounded[:, 128 * u : 128 * u + 128]
            grid_ref[pl.ds((a * 5 + u) * 64, 32), :] = pair
            grid_ref[pl.ds((a * 5 + u) * 64 + 32, 32), :] = pltpu.roll(pair, BLKW, 1)
        for j in range(ROWS):
            inc_buf[j, :, pl.ds(QUARTER * a, QUARTER)] = rounded[6 * j : 6 * j + 6].astype(BF16)
    inc_copy = pltpu.make_async_copy(inc_buf, inc_ref, inc_sem)
    inc_copy.start()
    for one in acc_refs:
        one[...] = jnp.zeros_like(one)
    across = lanes((BLKW, 128), 0).astype(F32)
    pair_code = lanes((64, 128), 0).astype(F32)
    slot_code = (lanes((1, 128), 1) // KOBS * 8).astype(F32)

    def look(d):
        fields = [obs_ref[pl.ds(d * 8 + f, 1), :] for f in range(6)]
        tiles = [grid_ref[pl.ds(place_smem[d * CAP + t], 8), :] for t in range(CAP)]
        offset = across - fields[5]
        table = jnp.where(offset == 3.0, fields[3], 0.0)
        for w in (2, 1, 0):
            table = jnp.where(offset == float(w), fields[w], table)
        hot = jnp.where(pair_code == fields[4] + slot_code, 1.0, 0.0).astype(BF16)
        blocks = jnp.concatenate(tiles, axis=0).T[:BLKW].astype(BF16)
        picks = jnp.dot(blocks, hot, preferred_element_type=F32)
        table_ref[d] = table
        hot_ref[d] = hot
        seen_ref[pl.ds(d, 1), :] = jnp.sum(picks * table, axis=0, keepdims=True)

    def add_back(d):
        back = (table_ref[d] * seen_ref[pl.ds(d, 1), :]).astype(BF16)
        spreads = lax.dot_general(hot_ref[d], back, NT, preferred_element_type=F32)
        for t in range(CAP):
            acc_refs[t % 4][pl.ds(place_smem[d * CAP + t], 8), pl.ds(0, BLKW)] += spreads[8 * t : 8 * t + 8]

    def in_groups(step):
        def group(k, carry):
            for d in range(GROUP):
                step(k * GROUP + d)
            return carry

        lax.fori_loop(0, N_LAT // GROUP, group, 0)

    in_groups(look)
    values = obs_ref[pl.ds(6, N_LAT, stride=8), :]
    scales = obs_ref[pl.ds(7, N_LAT, stride=8), :]
    seen_ref[...] = (seen_ref[...] - values) * scales
    in_groups(add_back)
    low = lanes((32, 128), 1) < BLKW

    def pair_of(u):
        left = sum(one[pl.ds(u * 64, 32), :] for one in acc_refs)
        right = sum(one[pl.ds(u * 64 + 32, 32), :] for one in acc_refs)
        return jnp.where(low, left, pltpu.roll(right, BLKW, 1))

    grads = [
        jnp.concatenate([pair_of(a * 5 + u) for u in range(5)], axis=1).astype(BF16).astype(F32) for a in range(4)
    ]
    even, other = grads[0] + grads[2], grads[1] + grads[3]
    folded = jnp.concatenate([even + other, even - other, grads[0] - grads[2], grads[1] - grads[3]], axis=0)
    back = lax.dot_general(folded.astype(BF16), phase_ref[...], NT, preferred_element_type=F32)
    for i in range(ORDERS):
        zero, two, odd, turned = masks[i]
        by_cos = back[:, i * DEVS : (i + 1) * DEVS]
        by_sin = back[:, (ORDERS + i) * DEVS : (ORDERS + i + 1) * DEVS]
        grouped_ref[2 * i] = by_cos[:32] * zero + by_cos[32:64] * two + by_cos[64:96] * odd + by_sin[96:] * turned
        grouped_ref[2 * i + 1] = by_sin[:32] * zero + by_sin[32:64] * two + by_sin[64:96] * odd - by_cos[96:] * turned
    for g in range(2 * ORDERS):
        for j in range(ROWS):
            turned_ref[pl.ds(64 * j + 6 * g, 6), :] = grouped_ref[g, pl.ds(6 * j, 6), :]
    for jj in range(3):
        wide_ref[pl.ds(jj, DEVS, stride=4), :] = turned_ref[pl.ds(128 * jj, 128), :].T
    for o in range(DEVS // N_LAT):
        wide_ref[pl.ds(4 * N_LAT * o + 3, N_LAT, stride=4), :] = seen_ref[...]
    out_ref[...] = wide_ref[...].astype(BF16)
    inc_copy.wait()


def analysis_kernel(
    order_ref, vertical_ref, control_ref, legendre_ref, rows_ref, weighted_ref, grad_ref,
    order_smem, vertical_buf, control_buf, table_ref, padded_ref, lookup_ref, coeffs_ref, wide_ref, turned_ref, half_ref, both_ref, small_sems, sems,
):
    small = start_small(order_ref, vertical_ref, control_ref, order_smem, vertical_buf, control_buf, small_sems)
    copies = start_tables(legendre_ref, table_ref, sems)
    wide_ref[...] = rows_ref[...].astype(F32)
    first = lax.axis_index("order") * (4 * N_LAT)
    weighted_ref[...] = wide_ref[pl.ds(first + 3, N_LAT, stride=4), :]
    for jj in range(3):
        turned_ref[pl.ds(128 * jj, 128), :] = wide_ref[pl.ds(jj, DEVS, stride=4), :].T
    for half in range(2):
        total = jnp.zeros((64, NHALF), F32)
        for j in range(ROWS):
            piece = turned_ref[pl.ds(64 * j, 64), pl.ds(128 * half, 128)].astype(BF16)
            total = total + jnp.dot(piece, row_picks(half, j), preferred_element_type=F32)
        half_ref[half] = total
    at = lanes((160, 64), 0)
    source = (at // 32) * 12 + (at % 16) // 2 * 2 + (at // 16) % 2
    twice = jnp.where((lanes((160, 64), 1) == source) & (at % 16 < 12), 1.0, 0.0).astype(BF16)
    for half in range(2):
        both_ref[half] = jnp.dot(twice, half_ref[half].astype(BF16), preferred_element_type=F32)
    for copy in small:
        copy.wait()
    padded_ref[...] = jnp.zeros_like(padded_ref)
    for a in range(2):
        for c in range(2):
            for f in range(3):
                padded_ref[pl.ds(16 * a + c * 6 + f * 2, 2), pl.ds(0, MM)] = vertical_buf[f, a]
    for i in range(ORDERS):
        lookup_ref[i] = lookup_rows(order_smem[first_slot() + i], padded_ref)
        for c in range(2):
            for f in range(3):
                coeffs_ref[i, pl.ds(c * 6 + f * 2, 2), :] = control_buf[c, f, i]
    signs = alternate_signs()
    for i in range(ORDERS):
        both = jnp.concatenate([both_ref[0, pl.ds(32 * i, 32), :], both_ref[1, pl.ds(32 * i, 32), :]], axis=0)
        copies[i].wait()
        sums = lax.dot_general(both.astype(BF16), table_ref[i], NT, preferred_element_type=F32)
        spectral = (sums[:32] + signs * sums[32:]) * lookup_ref[i]
        total = coeffs_ref[i] + (spectral[:16] + spectral[16:])
        for c in range(2):
            for f in range(3):
                at = c * 6 + f * 2
                grad_ref[c, f, i] = total[at : at + 2]


VMEM = pl.BlockSpec(memory_space=pltpu.VMEM)
SMEM = pl.BlockSpec(memory_space=pltpu.SMEM)
HBM = pl.BlockSpec(memory_space=pl.ANY)


def grant(mib):
    return pltpu.CompilerParams(vmem_limit_bytes=mib * 1024 * 1024)


def shards(
    control, vertical, legendre, order_assign, send_list, used_slot_counts, obs_count, obs_var, obs_col, obs_weight, obs_value, obs_error
):
    shape = jax.ShapeDtypeStruct
    with jax.named_scope("pack_obs"):
        packed, places = pl.pallas_call(
            pack_obs,
            out_shape=(shape((DEVS, 128), F32), shape((1, DEVS), jnp.int32)),
            in_specs=[VMEM] * 8,
            out_specs=(VMEM, VMEM),
            name="pack_obs",
        )(
            obs_var.reshape(N_LAT, 128), obs_col.reshape(N_LAT, 128), obs_weight.reshape(4, N_LAT, 128),
            obs_value.reshape(N_LAT, 128), obs_error.reshape(N_LAT, 128),
            used_slot_counts.reshape(1, N_LAT), obs_count.reshape(1, DEVS), send_list.reshape(1, DEVS),
        )
    obs = lax.all_to_all(packed.reshape(N_LAT, 8, 128), "lat", split_axis=0, concat_axis=0, tiled=True)
    coeffs = control.transpose(0, 1, 3, 2, 4)
    small_scratch = [
        pltpu.SMEM((MM,), jnp.int32),
        pltpu.VMEM(vertical.shape, F32),
        pltpu.VMEM(coeffs.shape, F32),
        pltpu.VMEM((ORDERS, MM, NHALF), BF16),
    ]
    with jax.named_scope("synthesis"):
        outgoing = pl.pallas_call(
            synth_kernel,
            out_shape=shape((4 * DEVS, 128), BF16),
            in_specs=[HBM] * 4,
            out_specs=VMEM,
            scratch_shapes=small_scratch
            + [
                pltpu.VMEM((16, 2 * MM + 128), F32),
                pltpu.VMEM((ORDERS, 24, MM), BF16),
                pltpu.VMEM((2, 64, NHALF), F32),
                pltpu.VMEM((4 * DEVS, 128), F32),
                pltpu.SemaphoreType.DMA((3,)),
                pltpu.SemaphoreType.DMA((ORDERS,)),
            ],
            compiler_params=grant(60),
            cost_estimate=pl.CostEstimate(flops=2 * 24 * 5 * MM * NHALF, bytes_accessed=9 << 20, transcendentals=0),
            name="synthesis",
        )(order_assign, vertical, coeffs, legendre)
    arrived = lax.all_to_all(
        outgoing.reshape(DEVS, 4, 128), ("order", "lat"), split_axis=0, concat_axis=0, tiled=True
    ).reshape(4 * DEVS, 128)
    by_device = order_assign.reshape(DEVS, ORDERS)
    with jax.named_scope("phases"):
        phases = pl.pallas_call(
            phase_kernel,
            out_shape=shape((2 * ORDERS * DEVS, QUARTER), BF16),
            in_specs=[VMEM],
            out_specs=VMEM,
            compiler_params=grant(16),
            cost_estimate=pl.CostEstimate(flops=40_000_000, bytes_accessed=4 << 20, transcendentals=0),
            name="phases",
        )(by_device)
    with jax.named_scope("middle"):
        increment, returning = pl.pallas_call(
            middle_kernel,
            out_shape=(shape((ROWS, VARS, NLON), BF16), shape((4 * DEVS, 128), BF16)),
            in_specs=[SMEM, VMEM, VMEM, VMEM, VMEM],
            out_specs=(HBM, VMEM),
            scratch_shapes=[
                pltpu.VMEM((4 * DEVS, 128), F32),
                pltpu.VMEM((384, DEVS), F32),
                pltpu.VMEM((2 * ORDERS, 32, DEVS), F32),
                pltpu.VMEM((128, 2 * ORDERS * DEVS), BF16),
                pltpu.VMEM((2 * CHUNKS * 32, 128), F32),
                [pltpu.VMEM((2 * CHUNKS * 32, 128), F32)] * 4,
                pltpu.VMEM((N_LAT, 128), F32),
                pltpu.VMEM((N_LAT, BLKW, 128), F32),
                pltpu.VMEM((N_LAT, 64, 128), BF16),
                pltpu.VMEM((ROWS, VARS, NLON), BF16),
                pltpu.SemaphoreType.DMA,
            ],
            compiler_params=grant(28),
            name="middle",
        )(places.reshape(DEVS), by_device.T, obs.reshape(DEVS, 128), arrived, phases)
    returned = lax.all_to_all(
        returning.reshape(DEVS, 4, 128), ("order", "lat"), split_axis=0, concat_axis=0, tiled=True
    ).reshape(4 * DEVS, 128)
    with jax.named_scope("analysis"):
        weighted, gradient = pl.pallas_call(
            analysis_kernel,
            out_shape=(shape((N_LAT, 128), F32), shape(coeffs.shape, F32)),
            in_specs=[HBM] * 4 + [VMEM],
            out_specs=(VMEM, VMEM),
            scratch_shapes=small_scratch
            + [
                pltpu.VMEM((32, 2 * MM + 128), F32),
                pltpu.VMEM((ORDERS, 32, MM), F32),
                pltpu.VMEM((ORDERS, 16, MM), F32),
                pltpu.VMEM((4 * DEVS, 128), F32),
                pltpu.VMEM((384, DEVS), F32),
                pltpu.VMEM((2, 64, NHALF), F32),
                pltpu.VMEM((2, 160, NHALF), F32),
                pltpu.SemaphoreType.DMA((3,)),
                pltpu.SemaphoreType.DMA((ORDERS,)),
            ],
            compiler_params=grant(60),
            name="analysis",
        )(order_assign, vertical, coeffs, legendre, returned)
    return increment, weighted.reshape(obs_value.shape), gradient.transpose(0, 1, 3, 2, 4)


def solution(mesh):
    return jax.shard_map(
        shards,
        mesh=mesh,
        in_specs=(
            P(None, None, None, ("order", "lat"), None),
            P(),
            P(("order", "lat"), None, None),
            P(),
            P("order", "lat", None),
            P("order", "lat", None),
            P("order", "lat", None),
            P("order", "lat", None),
            P("order", "lat", None),
            P(None, "order", "lat", None),
            P("order", "lat", None),
            P("order", "lat", None),
        ),
        out_specs=(
            P(("order", "lat"), None, None),
            P("order", "lat", None),
            P(None, None, None, ("order", "lat"), None),
        ),
        check_vma=False,
    )
```

```python
import functools
import math

import jax
import jax.numpy as jnp
from jax import lax
from jax.experimental import pallas as pl
from jax.experimental.pallas import tpu as pltpu
from jax.sharding import PartitionSpec as P

NLON = 2560
QUARTER = NLON // 4
BLKW = 64
CAP = 8
KOBS = 16
MM = 1280
NHALF = 640
VARS = 6
ROWS = 5
ORDERS = 5
DEVS = 256
GROUP = 32
N_LAT = 32
CHUNKS = NLON // 128
F32 = jnp.float32
BF16 = jnp.bfloat16
NT = (((1,), (1,)), ((), ()))


def lanes(shape, axis):
    return lax.broadcasted_iota(jnp.int32, shape, axis)


def pack_obs(var_ref, col_ref, weight_ref, value_ref, error_ref, used_ref, count_ref, send_ref, out_ref, place_ref):
    block = jnp.clip(send_ref[...], 0, 199)
    row = (block * 1639) >> 16
    place_ref[...] = (block - 40 * row) * 32 + row * 6
    source = lanes((N_LAT, DEVS), 0)
    slot = lanes((N_LAT, DEVS), 1)
    mine = jnp.where(slot // CAP == source, count_ref[...].astype(F32), 0.0).astype(BF16)
    spread = (lanes((DEVS, 128), 0) % CAP == lanes((DEVS, 128), 1) // KOBS).astype(F32).astype(BF16)
    counts = jnp.dot(mine, spread, preferred_element_type=F32)
    own = lanes((N_LAT, N_LAT), 0) == lanes((N_LAT, N_LAT), 1)
    used = jnp.sum(jnp.where(own, used_ref[...].astype(F32), 0.0), axis=1, keepdims=True)
    lane = lanes((N_LAT, 128), 1)
    live = ((lane // KOBS).astype(F32) < used) & ((lane % KOBS).astype(F32) < counts)
    fields = [weight_ref[w] for w in range(4)]
    fields.append(var_ref[...].astype(F32))
    fields.append(col_ref[...].astype(F32))
    fields.append(value_ref[...])
    fields.append(jnp.where(live, 1.0 / error_ref[...], 0.0))
    for index, field in enumerate(fields):
        out_ref[pl.ds(index, N_LAT, stride=8), :] = field


def row_picks(half, row):
    device = lanes((128, NHALF), 0)
    at = lanes((128, NHALF), 1)
    want = device * ROWS + row if half == 0 else (NHALF - 1 - row) - device * ROWS
    return jnp.where(at == want, 1.0, 0.0).astype(BF16)


def alternate_signs():
    return jnp.where(lanes((1, MM), 1) % 2 == 0, 1.0, -1.0)


def start_tables(legendre_ref, table_ref, sems):
    copies = [pltpu.make_async_copy(legendre_ref.at[i], table_ref.at[i], sems.at[i]) for i in range(ORDERS)]
    for copy in copies:
        copy.start(priority=1)
    return copies


def start_small(order_ref, vertical_ref, control_ref, order_smem, vertical_buf, control_buf, sems):
    copies = [
        pltpu.make_async_copy(order_ref, order_smem, sems.at[0]),
        pltpu.make_async_copy(vertical_ref, vertical_buf, sems.at[1]),
        pltpu.make_async_copy(control_ref, control_buf, sems.at[2]),
    ]
    for copy in copies:
        copy.start()
    return copies


def pad_vertical(vertical_buf, padded_ref):
    padded_ref[...] = jnp.zeros_like(padded_ref)
    for f in range(3):
        for a in range(2):
            padded_ref[pl.ds(f * 4 + a * 2, 2), pl.ds(0, MM)] = vertical_buf[f, a]


def lookup_rows(order, padded_ref):
    base = pl.multiple_of((order // 128) * 128, 128)
    window = padded_ref[:, pl.ds(base, MM + 128)]
    return pltpu.roll(window, (MM + 128) - order % 128, 1)[:, :MM]


def first_slot():
    return (lax.axis_index("order") * N_LAT + lax.axis_index("lat")) * ORDERS


def synth_kernel(
    order_ref, vertical_ref, control_ref, legendre_ref, out_ref,
    order_smem, vertical_buf, control_buf, table_ref, padded_ref, mixed_ref, half_ref, rows_ref, small_sems, sems,
):
    small = start_small(order_ref, vertical_ref, control_ref, order_smem, vertical_buf, control_buf, small_sems)
    copies = start_tables(legendre_ref, table_ref, sems)
    half_ref[...] = jnp.zeros_like(half_ref)
    for copy in small:
        copy.wait()
    pad_vertical(vertical_buf, padded_ref)
    signs = alternate_signs()
    for i in range(ORDERS):
        lookup = lookup_rows(order_smem[first_slot() + i], padded_ref)
        rows = []
        for c in range(2):
            for f in range(3):
                coeffs = control_buf[c, f, i]
                for a in range(2):
                    at = f * 4 + a * 2
                    rows.append(jnp.sum(lookup[at : at + 2] * coeffs, axis=0, keepdims=True))
        coeffs = jnp.concatenate(rows, axis=0)
        mixed_ref[i] = jnp.concatenate([coeffs, coeffs * signs], axis=0).astype(BF16)
    for i in range(ORDERS):
        copies[i].wait()
        both = jnp.dot(mixed_ref[i], table_ref[i], preferred_element_type=F32)
        half_ref[0, pl.ds(12 * i, 12), :] = both[:12]
        half_ref[1, pl.ds(12 * i, 12), :] = both[12:]
    low = lanes((128, 128), 1) < 64
    for half in range(2):
        rows = half_ref[half].astype(BF16)
        rows = jnp.concatenate([rows, rows], axis=0)
        picks = jnp.concatenate([row_picks(half, j) for j in range(ROWS)], axis=0)
        picked = lax.dot_general(picks, rows, NT, preferred_element_type=F32)
        picked = [picked[128 * j : 128 * j + 128] for j in range(ROWS)]
        picked.append(jnp.zeros_like(picked[0]))
        for jj in range(3):
            rows_ref[pl.ds(half * 512 + jj, 128, stride=4), :] = jnp.where(low, picked[2 * jj], picked[2 * jj + 1])
        rows_ref[pl.ds(half * 512 + 3, 128, stride=4), :] = jnp.zeros((128, 128), F32)
    out_ref[...] = rows_ref[...].astype(BF16)


def turn(steps):
    quadrant = jnp.floor(steps * (1.0 / QUARTER) + 0.5)
    angle = (steps - quadrant * QUARTER) * (2.0 * math.pi / NLON)
    square = angle * angle
    sine = angle * (
        1.0 + square * (-1.0 / 6 + square * (1.0 / 120 + square * (-1.0 / 5040 + square * (1.0 / 362880))))
    )
    cosine = 1.0 + square * (
        -0.5 + square * (1.0 / 24 + square * (-1.0 / 720 + square * (1.0 / 40320 - square * (1.0 / 3628800))))
    )
    part = quadrant - 4.0 * jnp.floor(quadrant * 0.25)
    odd = (part == 1.0) | (part == 3.0)
    cos_sign = jnp.where((part == 1.0) | (part == 2.0), -1.0, 1.0)
    sin_sign = jnp.where(part >= 2.0, -1.0, 1.0)
    return cos_sign * jnp.where(odd, sine, cosine), sin_sign * jnp.where(odd, cosine, sine)


def phase_kernel(order_ref, out_ref):
    lane = lanes((DEVS, 128), 1)
    coarse = jnp.zeros((DEVS, 128), F32)
    orders = [order_ref[:, i : i + 1].astype(F32) for i in range(ORDERS)]
    for i in range(ORDERS):
        coarse = jnp.where(lane // 5 == i, orders[i], coarse)
    weight = jnp.where(coarse == 0.0, 1.0, 2.0)
    coarse_cos, coarse_sin = turn(coarse * (128 * (lane % 5)).astype(F32))
    coarse_cos, coarse_sin = coarse_cos * weight, coarse_sin * weight
    lane = lane.astype(F32)
    for i in range(ORDERS):
        fine_cos, fine_sin = turn(orders[i] * lane)
        for a in range(QUARTER // 128):
            at = i * 5 + a
            big_cos, big_sin = coarse_cos[:, at : at + 1], coarse_sin[:, at : at + 1]
            out_ref[pl.ds(i * DEVS, DEVS), pl.ds(128 * a, 128)] = (fine_cos * big_cos - fine_sin * big_sin).astype(BF16)
            out_ref[pl.ds((ORDERS + i) * DEVS, DEVS), pl.ds(128 * a, 128)] = (
                -(fine_sin * big_cos + fine_cos * big_sin)
            ).astype(BF16)


def class_masks(order_row):
    residue = order_row % 4
    zero = jnp.where(residue == 0, 1.0, 0.0)
    two = jnp.where(residue == 2, 1.0, 0.0)
    odd = jnp.where(residue % 2 == 1, 1.0, 0.0)
    turned = jnp.where(residue == 1, 1.0, jnp.where(residue == 3, -1.0, 0.0))
    return zero, two, odd, turned


def middle_kernel(
    place_smem, order_ref, obs_ref, rows_ref, phase_ref, inc_ref, out_ref,
    wide_ref, turned_ref, grouped_ref, lhs_ref, grid_ref, acc_refs, seen_ref, table_ref, hot_ref, inc_buf, inc_sem,
):
    wide_ref[...] = rows_ref[...].astype(F32)
    for jj in range(3):
        turned_ref[pl.ds(128 * jj, 128), :] = wide_ref[pl.ds(jj, DEVS, stride=4), :].T
    grouped_ref[...] = jnp.zeros_like(grouped_ref)
    for g in range(2 * ORDERS):
        for j in range(ROWS):
            grouped_ref[g, pl.ds(6 * j, 6), :] = turned_ref[pl.ds(64 * j + 6 * g, 6), :]
    masks = [class_masks(order_ref[i : i + 1, :]) for i in range(ORDERS)]
    for i in range(ORDERS):
        zero, two, odd, turned = masks[i]
        real, imag = grouped_ref[2 * i], grouped_ref[2 * i + 1]
        by_cos = jnp.concatenate([real * zero, real * two, real * odd, imag * turned], axis=0)
        by_sin = jnp.concatenate([imag * zero, imag * two, imag * odd, -(real * turned)], axis=0)
        lhs_ref[:, pl.ds(i * DEVS, DEVS)] = by_cos.astype(BF16)
        lhs_ref[:, pl.ds((ORDERS + i) * DEVS, DEVS)] = by_sin.astype(BF16)
    sums = jnp.dot(lhs_ref[...], phase_ref[...], preferred_element_type=F32)
    r0, r2, ro, io = (sums[32 * k : 32 * k + 32] for k in range(4))
    even, skew = r0 + r2, r0 - r2
    quarters = [even + ro, skew - io, even - ro, skew + io]
    for a in range(4):
        rounded = quarters[a].astype(BF16).astype(F32)
        for u in range(5):
            pair = rounded[:, 128 * u : 128 * u + 128]
            grid_ref[pl.ds((a * 5 + u) * 64, 32), :] = pair
            grid_ref[pl.ds((a * 5 + u) * 64 + 32, 32), :] = pltpu.roll(pair, BLKW, 1)
        for j in range(ROWS):
            inc_buf[j, :, pl.ds(QUARTER * a, QUARTER)] = rounded[6 * j : 6 * j + 6].astype(BF16)
    inc_copy = pltpu.make_async_copy(inc_buf, inc_ref, inc_sem)
    inc_copy.start()
    for one in acc_refs:
        one[...] = jnp.zeros_like(one)
    across = lanes((BLKW, 128), 0).astype(F32)
    pair_code = lanes((64, 128), 0).astype(F32)
    slot_code = (lanes((1, 128), 1) // KOBS * 8).astype(F32)

    def look(d):
        fields = [obs_ref[pl.ds(d * 8 + f, 1), :] for f in range(6)]
        tiles = [grid_ref[pl.ds(place_smem[d * CAP + t], 8), :] for t in range(CAP)]
        offset = across - fields[5]
        table = jnp.where(offset == 3.0, fields[3], 0.0)
        for w in (2, 1, 0):
            table = jnp.where(offset == float(w), fields[w], table)
        hot = jnp.where(pair_code == fields[4] + slot_code, 1.0, 0.0).astype(BF16)
        blocks = jnp.concatenate(tiles, axis=0).T[:BLKW].astype(BF16)
        picks = jnp.dot(blocks, hot, preferred_element_type=F32)
        table_ref[d] = table
        hot_ref[d] = hot
        seen_ref[pl.ds(d, 1), :] = jnp.sum(picks * table, axis=0, keepdims=True)

    def add_back(d):
        back = (table_ref[d] * seen_ref[pl.ds(d, 1), :]).astype(BF16)
        spreads = lax.dot_general(hot_ref[d], back, NT, preferred_element_type=F32)
        for t in range(CAP):
            acc_refs[t % 4][pl.ds(place_smem[d * CAP + t], 8), pl.ds(0, BLKW)] += spreads[8 * t : 8 * t + 8]

    def in_groups(step):
        def group(k, carry):
            for d in range(GROUP):
                step(k * GROUP + d)
            return carry

        lax.fori_loop(0, N_LAT // GROUP, group, 0)

    in_groups(look)
    values = obs_ref[pl.ds(6, N_LAT, stride=8), :]
    scales = obs_ref[pl.ds(7, N_LAT, stride=8), :]
    seen_ref[...] = (seen_ref[...] - values) * scales
    in_groups(add_back)
    low = lanes((32, 128), 1) < BLKW

    def pair_of(u):
        left = sum(one[pl.ds(u * 64, 32), :] for one in acc_refs)
        right = sum(one[pl.ds(u * 64 + 32, 32), :] for one in acc_refs)
        return jnp.where(low, left, pltpu.roll(right, BLKW, 1))

    grads = [
        jnp.concatenate([pair_of(a * 5 + u) for u in range(5)], axis=1).astype(BF16).astype(F32) for a in range(4)
    ]
    even, other = grads[0] + grads[2], grads[1] + grads[3]
    folded = jnp.concatenate([even + other, even - other, grads[0] - grads[2], grads[1] - grads[3]], axis=0)
    back = lax.dot_general(folded.astype(BF16), phase_ref[...], NT, preferred_element_type=F32)
    for i in range(ORDERS):
        zero, two, odd, turned = masks[i]
        by_cos = back[:, i * DEVS : (i + 1) * DEVS]
        by_sin = back[:, (ORDERS + i) * DEVS : (ORDERS + i + 1) * DEVS]
        grouped_ref[2 * i] = by_cos[:32] * zero + by_cos[32:64] * two + by_cos[64:96] * odd + by_sin[96:] * turned
        grouped_ref[2 * i + 1] = by_sin[:32] * zero + by_sin[32:64] * two + by_sin[64:96] * odd - by_cos[96:] * turned
    for g in range(2 * ORDERS):
        for j in range(ROWS):
            turned_ref[pl.ds(64 * j + 6 * g, 6), :] = grouped_ref[g, pl.ds(6 * j, 6), :]
    for jj in range(3):
        wide_ref[pl.ds(jj, DEVS, stride=4), :] = turned_ref[pl.ds(128 * jj, 128), :].T
    for o in range(DEVS // N_LAT):
        wide_ref[pl.ds(4 * N_LAT * o + 3, N_LAT, stride=4), :] = seen_ref[...]
    out_ref[...] = wide_ref[...].astype(BF16)
    inc_copy.wait()


def analysis_kernel(
    order_ref, vertical_ref, control_ref, legendre_ref, rows_ref, weighted_ref, grad_ref,
    order_smem, vertical_buf, control_buf, table_ref, padded_ref, lookup_ref, coeffs_ref, wide_ref, turned_ref, half_ref, both_ref, small_sems, sems,
):
    small = start_small(order_ref, vertical_ref, control_ref, order_smem, vertical_buf, control_buf, small_sems)
    copies = start_tables(legendre_ref, table_ref, sems)
    wide_ref[...] = rows_ref[...].astype(F32)
    weighted = wide_ref[pl.ds(3, N_LAT, stride=4), :]
    for o in range(1, DEVS // N_LAT):
        mine = lax.axis_index("order") == o
        weighted = jnp.where(mine, wide_ref[pl.ds(4 * N_LAT * o + 3, N_LAT, stride=4), :], weighted)
    weighted_ref[...] = weighted
    for jj in range(3):
        turned_ref[pl.ds(128 * jj, 128), :] = wide_ref[pl.ds(jj, DEVS, stride=4), :].T
    for half in range(2):
        total = jnp.zeros((64, NHALF), F32)
        for j in range(ROWS):
            piece = turned_ref[pl.ds(64 * j, 64), pl.ds(128 * half, 128)].astype(BF16)
            total = total + jnp.dot(piece, row_picks(half, j), preferred_element_type=F32)
        half_ref[half] = total
    at = lanes((160, 64), 0)
    source = (at // 32) * 12 + (at % 16) // 2 * 2 + (at // 16) % 2
    twice = jnp.where((lanes((160, 64), 1) == source) & (at % 16 < 12), 1.0, 0.0).astype(BF16)
    for half in range(2):
        both_ref[half] = jnp.dot(twice, half_ref[half].astype(BF16), preferred_element_type=F32)
    for copy in small:
        copy.wait()
    padded_ref[...] = jnp.zeros_like(padded_ref)
    for a in range(2):
        for c in range(2):
            for f in range(3):
                padded_ref[pl.ds(16 * a + c * 6 + f * 2, 2), pl.ds(0, MM)] = vertical_buf[f, a]
    for i in range(ORDERS):
        lookup_ref[i] = lookup_rows(order_smem[first_slot() + i], padded_ref)
        for c in range(2):
            for f in range(3):
                coeffs_ref[i, pl.ds(c * 6 + f * 2, 2), :] = control_buf[c, f, i]
    signs = alternate_signs()
    for i in range(ORDERS):
        both = jnp.concatenate([both_ref[0, pl.ds(32 * i, 32), :], both_ref[1, pl.ds(32 * i, 32), :]], axis=0)
        copies[i].wait()
        sums = lax.dot_general(both.astype(BF16), table_ref[i], NT, preferred_element_type=F32)
        spectral = (sums[:32] + signs * sums[32:]) * lookup_ref[i]
        total = coeffs_ref[i] + (spectral[:16] + spectral[16:])
        for c in range(2):
            for f in range(3):
                at = c * 6 + f * 2
                grad_ref[c, f, i] = total[at : at + 2]


VMEM = pl.BlockSpec(memory_space=pltpu.VMEM)
SMEM = pl.BlockSpec(memory_space=pltpu.SMEM)
HBM = pl.BlockSpec(memory_space=pl.ANY)


def grant(mib):
    return pltpu.CompilerParams(vmem_limit_bytes=mib * 1024 * 1024)


def shards(
    control, vertical, legendre, order_assign, send_list, used_slot_counts, obs_count, obs_var, obs_col, obs_weight, obs_value, obs_error
):
    shape = jax.ShapeDtypeStruct
    with jax.named_scope("pack_obs"):
        packed, places = pl.pallas_call(
            pack_obs,
            out_shape=(shape((DEVS, 128), F32), shape((1, DEVS), jnp.int32)),
            in_specs=[VMEM] * 8,
            out_specs=(VMEM, VMEM),
            name="pack_obs",
        )(
            obs_var.reshape(N_LAT, 128), obs_col.reshape(N_LAT, 128), obs_weight.reshape(4, N_LAT, 128),
            obs_value.reshape(N_LAT, 128), obs_error.reshape(N_LAT, 128),
            used_slot_counts.reshape(1, N_LAT), obs_count.reshape(1, DEVS), send_list.reshape(1, DEVS),
        )
    obs = lax.all_to_all(packed.reshape(N_LAT, 8, 128), "lat", split_axis=0, concat_axis=0, tiled=True)
    coeffs = control.transpose(0, 1, 3, 2, 4)
    small_scratch = [
        pltpu.SMEM((MM,), jnp.int32),
        pltpu.VMEM(vertical.shape, F32),
        pltpu.VMEM(coeffs.shape, F32),
        pltpu.VMEM((ORDERS, MM, NHALF), BF16),
    ]
    with jax.named_scope("synthesis"):
        outgoing = pl.pallas_call(
            synth_kernel,
            out_shape=shape((4 * DEVS, 128), BF16),
            in_specs=[HBM] * 4,
            out_specs=VMEM,
            scratch_shapes=small_scratch
            + [
                pltpu.VMEM((16, 2 * MM + 128), F32),
                pltpu.VMEM((ORDERS, 24, MM), BF16),
                pltpu.VMEM((2, 64, NHALF), F32),
                pltpu.VMEM((4 * DEVS, 128), F32),
                pltpu.SemaphoreType.DMA((3,)),
                pltpu.SemaphoreType.DMA((ORDERS,)),
            ],
            compiler_params=grant(60),
            cost_estimate=pl.CostEstimate(flops=2 * 24 * 5 * MM * NHALF, bytes_accessed=9 << 20, transcendentals=0),
            name="synthesis",
        )(order_assign, vertical, coeffs, legendre)
    arrived = lax.all_to_all(
        outgoing.reshape(DEVS, 4, 128), ("order", "lat"), split_axis=0, concat_axis=0, tiled=True
    ).reshape(4 * DEVS, 128)
    by_device = order_assign.reshape(DEVS, ORDERS)
    with jax.named_scope("phases"):
        phases = pl.pallas_call(
            phase_kernel,
            out_shape=shape((2 * ORDERS * DEVS, QUARTER), BF16),
            in_specs=[VMEM],
            out_specs=VMEM,
            compiler_params=grant(16),
            cost_estimate=pl.CostEstimate(flops=40_000_000, bytes_accessed=4 << 20, transcendentals=0),
            name="phases",
        )(by_device)
    with jax.named_scope("middle"):
        increment, returning = pl.pallas_call(
            middle_kernel,
            out_shape=(shape((ROWS, VARS, NLON), BF16), shape((4 * DEVS, 128), BF16)),
            in_specs=[SMEM, VMEM, VMEM, VMEM, VMEM],
            out_specs=(HBM, VMEM),
            scratch_shapes=[
                pltpu.VMEM((4 * DEVS, 128), F32),
                pltpu.VMEM((384, DEVS), F32),
                pltpu.VMEM((2 * ORDERS, 32, DEVS), F32),
                pltpu.VMEM((128, 2 * ORDERS * DEVS), BF16),
                pltpu.VMEM((2 * CHUNKS * 32, 128), F32),
                [pltpu.VMEM((2 * CHUNKS * 32, 128), F32)] * 4,
                pltpu.VMEM((N_LAT, 128), F32),
                pltpu.VMEM((N_LAT, BLKW, 128), F32),
                pltpu.VMEM((N_LAT, 64, 128), BF16),
                pltpu.VMEM((ROWS, VARS, NLON), BF16),
                pltpu.SemaphoreType.DMA,
            ],
            compiler_params=grant(28),
            name="middle",
        )(places.reshape(DEVS), by_device.T, obs.reshape(DEVS, 128), arrived, phases)
    returned = lax.all_to_all(
        returning.reshape(DEVS, 4, 128), ("order", "lat"), split_axis=0, concat_axis=0, tiled=True
    ).reshape(4 * DEVS, 128)
    with jax.named_scope("analysis"):
        weighted, gradient = pl.pallas_call(
            analysis_kernel,
            out_shape=(shape((N_LAT, 128), F32), shape(coeffs.shape, F32)),
            in_specs=[HBM] * 4 + [VMEM],
            out_specs=(VMEM, VMEM),
            scratch_shapes=small_scratch
            + [
                pltpu.VMEM((32, 2 * MM + 128), F32),
                pltpu.VMEM((ORDERS, 32, MM), F32),
                pltpu.VMEM((ORDERS, 16, MM), F32),
                pltpu.VMEM((4 * DEVS, 128), F32),
                pltpu.VMEM((384, DEVS), F32),
                pltpu.VMEM((2, 64, NHALF), F32),
                pltpu.VMEM((2, 160, NHALF), F32),
                pltpu.SemaphoreType.DMA((3,)),
                pltpu.SemaphoreType.DMA((ORDERS,)),
            ],
            compiler_params=grant(60),
            name="analysis",
        )(order_assign, vertical, coeffs, legendre, returned)
    return increment, weighted.reshape(obs_value.shape), gradient.transpose(0, 1, 3, 2, 4)


def solution(mesh):
    return jax.shard_map(
        shards,
        mesh=mesh,
        in_specs=(
            P(None, None, None, ("order", "lat"), None),
            P(),
            P(("order", "lat"), None, None),
            P(),
            P("order", "lat", None),
            P("order", "lat", None),
            P("order", "lat", None),
            P("order", "lat", None),
            P("order", "lat", None),
            P(None, "order", "lat", None),
            P("order", "lat", None),
            P("order", "lat", None),
        ),
        out_specs=(
            P(("order", "lat"), None, None),
            P("order", "lat", None),
            P(None, None, None, ("order", "lat"), None),
        ),
        check_vma=False,
    )
```
